256 devices in a mesh: box: 128 (over x, y, z_lo, core), shift: 2 (over z_hi).
Axes of the slice: x: 4, y: 4, z: 8 (z_hi: 2, z_lo: 4; z = z_hi * 4 + z_lo), core: 2. Of those that a mesh axis runs over, the one named last changes fastest.
Arguments:
- vectors: bfloat16 [2, 8192, 128, 128], P('shift', 'box'), may hold values from -6 to 6
- sigma: float32 [2, 2], P('shift'), may hold values from 0.5 to 2
- near_blocks: bfloat16 [8192, 6, 128, 128], P('box', None, 'shift'), may hold values from -0.21875 to 0.21875
- near_index: int32 [8192, 6], P('box'), may hold values from -1 to 8191, as said below
- radiate: bfloat16 [128, 128], replicated, may hold values from -0.5 to 0.5
- interp_one: bfloat16 [8, 512, 128], replicated, may hold values from -0.1875 to 0.1875
- interp_two: bfloat16 [8, 2048, 512], replicated, may hold values from -0.09375 to 0.09375
- trans_one: float32 [316, 512], replicated, may hold values from -1.5 to 1.5
- level1_source: int32 [1024, 16], P('box'), may hold values from -1 to 1023, as said below
- level1_offset: int32 [1024, 16], P('box'), may hold values from 0 to 315
- trans_two: float32 [316, 2048], P(None, 'box'), may hold values from -1 to 1
- level2_source: int32 [128, 32], replicated, may hold values from -1 to 127, as said below
- level2_offset: int32 [128, 32], replicated, may hold values from 0 to 315
Outputs:
- applied: float32 [2, 8192, 128, 128], P('shift', 'box')
The draws below stay inside these ranges and needn't reach their ends.
Inputs may be any that keep to these rules, and one draw needn't show every extreme that they name: `near_index`: leaf boxes are numbered along a space-filling curve. Entry 0 of each row is the box itself; every live entry names a box within 64 of the row's box; live entries come first, unused ones are -1; some rows use all 6 entries and some only one. `level1_source`: entry 0 of each row is live; every live entry names a box within 8 of the row's box; live entries come first, unused ones are -1; some rows use all 16 entries and some only one. `level2_source`: entry 0 of each row is live; live entries come first, unused ones are -1; some rows use all 32 entries and some only one.
All inputs are finite; a program needn't handle non-finite values.
Results may differ from the reference program's by a relative error of at most 0.0035.
Values may be sent and summed in bfloat16 or wider, within the bound.
A program may use at most 192 MiB of HBM per device.

```python
import jax
import jax.numpy as jnp
from jax import lax

U = 128
K0R = 128
K1R = 512
K2R = 2048
R = 128
BOX_DEV = 64
NN = 6
M1 = 16
M2 = 32
NOFF = 316
SHIFTS = 2
NB = 8192
NB1 = 1024
NB2 = 128


def ragged_lists(key, rows_total, width, reach):
    key_count = jax.random.fold_in(key, 11)
    key_step = jax.random.fold_in(key, 12)
    rows = jnp.arange(rows_total)
    count = jax.random.randint(key_count, (rows_total,), 1, width + 1)
    count = jnp.where(rows % 16 == 0, width, count)
    count = jnp.where(rows % 16 == 8, 1, count)
    step = jax.random.randint(key_step, (rows_total, width), -reach, reach + 1)
    step = step.at[:, 0].set(jnp.abs(step[:, 0]))
    ids = jnp.clip(rows[:, None] + step, 0, rows_total - 1)
    slots = jnp.arange(width)[None, :]
    return (ids, slots < count[:, None])


def draw_near_index(key, part):
    ids, live = ragged_lists(key, NB, NN, BOX_DEV)
    ids = ids.at[:, 0].set(jnp.arange(NB))
    return jnp.where(live, ids, -1).astype(jnp.int32)


def draw_level1_source(key, part):
    ids, live = ragged_lists(key, NB1, M1, BOX_DEV // 8)
    return jnp.where(live, ids, -1).astype(jnp.int32)


def draw_level2_source(key, part):
    ids, live = ragged_lists(key, NB2, M2, 1)
    far_ids = jax.random.randint(jax.random.fold_in(key, 13), (NB2, M2), 0, NB2)
    rows = jnp.arange(NB2)
    far_ids = far_ids.at[:, 0].set((rows + NB2 // 2) % NB2)
    return jnp.where(live, far_ids, -1).astype(jnp.int32)


def touch_ends(entries, key, least, high):
    index_at = [jax.random.randint(jax.random.fold_in(key, axis), (), 0, length) for axis, length in enumerate(entries.shape)]
    longest = entries.shape.index(max(entries.shape))
    beside = index_at[:longest] + [(index_at[longest] + 1) % entries.shape[longest]] + index_at[longest + 1:]
    return entries.at[tuple(index_at)].set(least).at[tuple(beside)].set(high)


def level_of(key, shape, shards, least, high):
    def one(dim, parts):
        heights = jax.random.uniform(jax.random.fold_in(jax.random.fold_in(key, 6), dim), (parts,), jnp.float32, least / len(shards), high / len(shards))
        return jnp.repeat(jnp.exp(heights), shape[dim] // parts).reshape((-1,) + (1,) * (len(shape) - dim - 1))

    factor_of = one(*shards[0])
    for cut in shards[1:]:
        factor_of = factor_of * one(*cut)
    return factor_of


def centred(key, shape, scale, limit, cuts=(), kind=jnp.bfloat16):
    gain = level_of(key, shape, cuts, -0.22, 0.18) if cuts else 1.0
    result = jax.random.normal(key, shape, jnp.float32) * scale * gain
    return jnp.minimum(jnp.maximum(result, -limit), limit).astype(kind)


def setup_inputs(seed: int = 0) -> dict:
    key_of = jax.random.split(jax.random.key(seed), 14)
    vectors = centred(key_of[0], (SHIFTS, NB, U, R), 1.0, 6.0, ((0, 2), (1, 128)))
    sigma = jnp.clip(0.5 + 1.5 * jax.random.uniform(key_of[1], (SHIFTS, 2), jnp.float32) ** level_of(key_of[1], (SHIFTS, 2), ((0, 2),), -0.2, 0.2), 0.5, 2.0)
    near_blocks = centred(key_of[2], (NB, NN, U, U), (U * NN) ** -0.5, 0.21875, ((0, 128), (2, 2)))
    near_index = draw_near_index(jax.random.fold_in(key_of[13], 71), 0)
    radiate = centred(key_of[4], (K0R, U), U ** -0.5, 0.5)
    interp_one = centred(key_of[5], (8, K1R, K0R), (8 * K0R) ** -0.5, 0.1875)
    interp_two = centred(key_of[6], (8, K2R, K1R), (8 * K1R) ** -0.5, 0.09375)
    trans_one = centred(key_of[7], (NOFF, K1R), M1 ** -0.5, 1.5, (), jnp.float32)
    level1_source = draw_level1_source(jax.random.fold_in(key_of[13], 71), 0)
    level1_offset = touch_ends(jax.random.randint(key_of[9], (NB1, M1), 0, NOFF), jax.random.fold_in(key_of[9], 1), 0, NOFF - 1).astype(jnp.int32)
    trans_two = centred(key_of[10], (NOFF, K2R), M2 ** -0.5, 1.0, ((1, 128),), jnp.float32)
    level2_source = draw_level2_source(jax.random.fold_in(key_of[13], 71), 0)
    level2_offset = touch_ends(jax.random.randint(key_of[12], (NB2, M2), 0, NOFF), jax.random.fold_in(key_of[12], 1), 0, NOFF - 1).astype(jnp.int32)
    return dict(vectors=vectors, sigma=sigma, near_blocks=near_blocks, near_index=near_index, radiate=radiate, interp_one=interp_one, interp_two=interp_two, trans_one=trans_one, level1_source=level1_source, level1_offset=level1_offset, trans_two=trans_two, level2_source=level2_source, level2_offset=level2_offset)


def near_product(field, near_blocks, near_index):
    groups = NB // BOX_DEV
    blocks = near_blocks.reshape(groups, BOX_DEV, NN, U, U)
    ids = near_index.reshape(groups, BOX_DEV, NN)

    def one_group(pair):
        block_part, id_part = pair
        live = id_part >= 0
        safe = jnp.where(live, id_part, 0).astype(jnp.int32)
        source = field[safe] * live[:, :, None, None].astype(field.dtype)
        return jnp.einsum('bjvu,bjur->bvr', block_part.astype(jnp.float32), source.astype(jnp.float32))

    return lax.map(one_group, (blocks, ids)).reshape(NB, U, R)


def translate(pattern, table, offsets, sources):
    def one_box(pair):
        off_row, src_row = pair
        live = src_row >= 0
        safe = jnp.where(live, src_row, 0).astype(jnp.int32)
        weights = table[off_row] * live[:, None].astype(jnp.float32)
        return jnp.einsum('jk,jkr->kr', weights, pattern[safe].astype(jnp.float32))

    return lax.map(one_box, (offsets, sources))


def reference(vectors, sigma, near_blocks, near_index, radiate, interp_one, interp_two, trans_one, level1_source, level1_offset, trans_two, level2_source, level2_offset):
    results = []
    for shift_id in range(SHIFTS):
        field = vectors[shift_id]
        near = near_product(field, near_blocks, near_index)
        leaf = jnp.einsum('ku,bur->bkr', radiate.astype(jnp.float32), field.astype(jnp.float32)).astype(jnp.bfloat16)
        upper = jnp.einsum('oqk,cokr->cqr', interp_one.astype(jnp.float32), leaf.reshape(NB1, 8, K0R, R).astype(jnp.float32)).astype(jnp.bfloat16)
        coarse = jnp.einsum('oqk,gokr->gqr', interp_two.astype(jnp.float32), upper.reshape(NB2, 8, K1R, R).astype(jnp.float32)).astype(jnp.bfloat16)
        incoming = translate(coarse, trans_two, level2_offset, level2_source).astype(jnp.bfloat16)
        across = translate(upper, trans_one, level1_offset, level1_source)
        down = jnp.einsum('oqk,gqr->gokr', interp_two.astype(jnp.float32), incoming.astype(jnp.float32)).reshape(NB1, K1R, R)
        local_in = (across + down).astype(jnp.bfloat16)
        leaf_in = jnp.einsum('oqk,cqr->cokr', interp_one.astype(jnp.float32), local_in.astype(jnp.float32)).reshape(NB, K0R, R).astype(jnp.bfloat16)
        far = jnp.einsum('ku,bkr->bur', radiate.astype(jnp.float32), leaf_in.astype(jnp.float32))
        real_part = field[:, : U // 2].astype(jnp.float32)
        imag_part = field[:, U // 2:].astype(jnp.float32)
        sig_re = sigma[shift_id, 0]
        sig_im = sigma[shift_id, 1]
        scaled = jnp.concatenate([sig_re * real_part - sig_im * imag_part, sig_re * imag_part + sig_im * real_part], axis=1)
        results.append(near + far - scaled)
    return jnp.stack(results)
```

```python
import functools

import jax
import jax.numpy as jnp
from jax import lax
from jax.experimental import pallas as pl
from jax.experimental.pallas import tpu as pltpu
from jax.sharding import PartitionSpec as P

BF = jnp.bfloat16
F32 = jnp.float32
MIB = 1 << 20
ANY = pl.BlockSpec(memory_space=pl.ANY)
VMEM = pl.BlockSpec(memory_space=pltpu.VMEM)
BOTH = ("box", "shift")
DEPTH = 4


def dot(a, b):
    return jnp.dot(a, b, preferred_element_type=F32)


def dot_nt(a, b):
    return lax.dot_general(a, b, (((1,), (1,)), ((), ())), preferred_element_type=F32)


def routes(boxes):
    chips = boxes // 2

    def flat(chip, core, shift):
        return (chip % chips * 2 + core) * 2 + shift

    hops = ([], [], [])
    for chip in range(chips):
        for core in range(2):
            wraps = chip % DEPTH == (DEPTH - 1 if core else 0)
            beside = chip + (1 if core else -1)
            for shift in range(2):
                stops = [
                    flat(chip, core, shift),
                    flat(beside, 1 - core, 1 - shift if wraps else shift),
                    flat(chip, core, 1 - shift),
                    flat(beside, 1 - core, shift if wraps else 1 - shift),
                ]
                for hop in range(3):
                    hops[hop].append((stops[hop], stops[hop + 1]))
    return hops


def place():
    me = lax.axis_index("box")
    core = lax.rem(me, 2)
    depth = lax.rem(lax.div(me, 2), DEPTH)
    wraps = jnp.where(core == 0, depth == 0, depth == DEPTH - 1).astype(jnp.int32)
    return me, core, wraps


def exchange_kernel(count, x_ref, o_ref, send, recv, local):
    me = lax.axis_index("box")
    shift = lax.axis_index("shift")
    own = pltpu.make_async_copy(x_ref.at[me], o_ref.at[me], local)
    own.start()

    @pl.loop(1, count)
    def _(step):
        other = lax.rem(me + step, count)
        pltpu.make_async_remote_copy(
            x_ref.at[other],
            o_ref.at[me],
            send,
            recv,
            device_id=(other, shift),
            device_id_type=pl.DeviceIdType.MESH,
        ).start()

    own.wait()
    rest = pl.ds(0, count - 1)
    pltpu.make_async_copy(x_ref.at[rest], x_ref.at[rest], send).wait()
    pltpu.make_async_copy(o_ref.at[rest], o_ref.at[rest], recv).wait()


def exchange(blocks):
    count = blocks.shape[0]
    return pl.pallas_call(
        functools.partial(exchange_kernel, count),
        out_shape=jax.ShapeDtypeStruct(blocks.shape, BF),
        in_specs=[VMEM],
        out_specs=VMEM,
        scratch_shapes=[pltpu.SemaphoreType.DMA] * 3,
        compiler_params=pltpu.CompilerParams(has_side_effects=True),
        cost_estimate=pl.CostEstimate(flops=0, bytes_accessed=64 * MIB, transcendentals=0),
        name="exchange",
    )(blocks)


def parent_pattern(x_of, radiate, one_ref):
    total = None
    for pair in range(4):
        leaves = [dot(radiate, x_of(2 * pair + i)).astype(BF) for i in range(2)]
        lhs = jnp.concatenate([one_ref[2 * pair], one_ref[2 * pair + 1]], axis=1)
        term = dot(lhs, jnp.concatenate(leaves, axis=0))
        total = term if total is None else total + term
    return total


def upward_kernel(x_ref, radiate_ref, one_ref, two_ref, coarse_ref, total):
    step = pl.program_id(0)
    upper = parent_pattern(lambda i: x_ref[i], radiate_ref[...], one_ref).astype(BF)
    term = dot(two_ref[0], upper)

    @pl.when(step == 0)
    def _():
        total[...] = term

    @pl.when(step > 0)
    def _():
        total[...] += term

    @pl.when(step == pl.num_programs(0) - 1)
    def _():
        coarse_ref[...] = total[...].astype(BF)


def upward(x, radiate, one, two):
    octants, k2, k1 = two.shape
    _, u, r = x.shape
    return pl.pallas_call(
        upward_kernel,
        grid=(octants,),
        out_shape=jax.ShapeDtypeStruct((k2, r), BF),
        in_specs=[
            pl.BlockSpec((8, u, r), lambda i: (i, 0, 0)),
            VMEM,
            VMEM,
            pl.BlockSpec((1, k2, k1), lambda i: (i, 0, 0)),
        ],
        out_specs=pl.BlockSpec((k2, r), lambda i: (0, 0)),
        scratch_shapes=[pltpu.VMEM((k2, r), F32)],
        compiler_params=pltpu.CompilerParams(vmem_limit_bytes=24 * MIB),
        cost_estimate=pl.CostEstimate(flops=7_000_000_000, bytes_accessed=40 * MIB, transcendentals=0),
        name="upward",
    )(x, radiate, one, two)


def translate_kernel(width, source_ref, offset_ref, coarse_ref, weight_ref, out_ref):
    @pl.loop(0, out_ref.shape[0])
    def _(box):
        total = jnp.zeros(out_ref.shape[1:], F32)
        for j in range(width):
            at = box * width + j
            total += weight_ref[offset_ref[at]] * coarse_ref[source_ref[at]].astype(F32)
        out_ref[box] = total.astype(BF)


def translate(coarse, table, source, offset):
    boxes, width = source.shape
    classes, samples = table.shape
    live = source >= 0
    weights = jnp.broadcast_to(
        jnp.pad(table, ((0, 1), (0, 0)))[:, :, None], (classes + 1, samples, coarse.shape[2])
    )
    return pl.pallas_call(
        functools.partial(translate_kernel, width),
        out_shape=jax.ShapeDtypeStruct(coarse.shape, BF),
        grid_spec=pltpu.PrefetchScalarGridSpec(
            num_scalar_prefetch=2, grid=(), in_specs=[VMEM, VMEM], out_specs=VMEM
        ),
        compiler_params=pltpu.CompilerParams(vmem_limit_bytes=16 * MIB),
        cost_estimate=pl.CostEstimate(flops=2_000_000_000, bytes_accessed=40 * MIB, transcendentals=0),
        name="translate",
    )(
        jnp.where(live, source, 0).reshape(-1),
        jnp.where(live, offset, classes).reshape(-1),
        coarse,
        weights,
    )


def near_kernel(
    group, slots, index_ref, blocks_ref, x, mate, first, partner, partner_mate, last,
    own_ref, other_ref, held, sems,
):
    step = pl.program_id(0)
    me, core, wraps = place()
    count = x.shape[0]

    @pl.when(step == 0)
    def _():
        towards = 2 * core
        within = 2 - towards
        moves = (
            (x, 0, 1),
            (mate, 0, within),
            (first, wraps, towards),
            (partner, 1, 1),
            (partner_mate, 1, within),
            (last, 1 - wraps, towards),
        )
        copies = [
            pltpu.make_async_copy(src, held.at[kind, pl.ds(slot * count, count)], sems.at[i])
            for i, (src, kind, slot) in enumerate(moves)
        ]
        for copy in copies:
            copy.start()
        zero = jnp.zeros(held.shape[2:], BF)
        held[0, 3 * count] = zero
        held[1, 3 * count] = zero
        for copy in copies:
            copy.wait()

    base = me * count - count
    for b in range(group):
        total = None
        for pair in range(slots // 2):
            rows = []
            for i in range(2):
                at = index_ref[(step * group + b) * slots + 2 * pair + i]
                at = jnp.where(at >= 0, at - base, 3 * count)
                rows.append(jnp.concatenate([held[0, at], held[1, at]], axis=1))
            lhs = jnp.concatenate([blocks_ref[b, 2 * pair], blocks_ref[b, 2 * pair + 1]], axis=1)
            term = dot(lhs, jnp.concatenate(rows, axis=0))
            total = term if total is None else total + term
        r = own_ref.shape[2]
        own_ref[b] = total[:, :r]
        other_ref[b] = total[:, r:].astype(BF)


def near_field(index, blocks, *vectors):
    count, slots, half, u = blocks.shape
    r = vectors[0].shape[2]
    group = 8
    out = pl.BlockSpec((group, half, r), lambda i, _: (i, 0, 0))
    return pl.pallas_call(
        functools.partial(near_kernel, group, slots),
        out_shape=[
            jax.ShapeDtypeStruct((count, half, r), F32),
            jax.ShapeDtypeStruct((count, half, r), BF),
        ],
        grid_spec=pltpu.PrefetchScalarGridSpec(
            num_scalar_prefetch=1,
            grid=(count // group,),
            in_specs=[pl.BlockSpec((group, slots, half, u), lambda i, _: (i, 0, 0, 0))] + [ANY] * 6,
            out_specs=[out, out],
            scratch_shapes=[
                pltpu.VMEM((2, 3 * count + 1, u, r), BF),
                pltpu.SemaphoreType.DMA((6,)),
            ],
        ),
        compiler_params=pltpu.CompilerParams(vmem_limit_bytes=32 * MIB),
        cost_estimate=pl.CostEstimate(flops=6_000_000_000, bytes_accessed=30 * MIB, transcendentals=0),
        name="near_field",
    )(index.reshape(-1), blocks, *vectors)


def downward_kernel(
    width, source_ref, offset_ref, x, mate, first, last, own_ref, sigma_ref, radiate_ref, turned_ref,
    one_ref, two_ref, table_ref, incoming_ref, base_ref, held, patterns, flat, weights, across, sems,
):
    step = pl.program_id(0)
    me, core, wraps = place()
    count, u, r = x.shape
    parents = count // 8
    eye = (
        lax.broadcasted_iota(jnp.int32, (r, r), 0) == lax.broadcasted_iota(jnp.int32, (r, r), 1)
    ).astype(BF)

    @pl.when(step == 0)
    def _():
        towards = 2 * core
        within = 2 - towards
        beside = pl.ds(towards * count, count)
        pltpu.make_async_copy(x, held.at[pl.ds(count, count)], sems.at[0]).start()
        pltpu.make_async_copy(mate, held.at[pl.ds(within * count, count)], sems.at[1]).start()

        @pl.when(wraps == 0)
        def _():
            pltpu.make_async_copy(first, held.at[beside], sems.at[2]).start()

        @pl.when(wraps == 1)
        def _():
            pltpu.make_async_copy(last, held.at[beside], sems.at[2]).start()

        flat[...] = dot_nt(eye, incoming_ref[...]).astype(BF)
        for i in range(3):
            pltpu.make_async_copy(x, held.at[pl.ds(count, count)], sems.at[i]).wait()

        @pl.loop(0, 3 * parents)
        def _(c):
            upper = parent_pattern(lambda i: held[c * 8 + i], radiate_ref[...], one_ref).astype(BF)
            patterns[c] = dot_nt(eye, upper).astype(BF)

    origin = me * parents - parents
    at = []
    for j in range(width):
        source = source_ref[step * width + j]
        live = source >= 0
        at.append(jnp.where(live, source - origin, 0))
        row = table_ref[pl.ds(offset_ref[step * width + j], 1), :]
        weights[pl.ds(j, 1), :] = row * live.astype(F32)

    @pl.loop(0, r // 16)
    def _(part):
        rows = pl.ds(part * 16, 16)
        total = None
        for j in range(width):
            term = weights[pl.ds(j, 1), :] * patterns[at[j], rows, :].astype(F32)
            total = term if total is None else total + term
        across[rows, :] = total

    local = (across[...] + dot(flat[...], two_ref[0])).astype(BF)
    shift = lax.axis_index("shift")
    half = u // 2
    sig_re, sig_im = sigma_ref[0], sigma_ref[1]
    for child in range(8):
        leaf_in = dot(local, one_ref[child]).astype(BF)
        far = dot_nt(turned_ref[...], leaf_in)
        field = held[count + step * 8 + child].astype(F32)
        real, imag = field[:half], field[half:]
        base_ref[child, :half] = far[:half] - (sig_re * real - sig_im * imag)
        base_ref[child, half:] = far[half:] - (sig_re * imag + sig_im * real)
        mine = pl.ds(pl.multiple_of(shift * half, half), half)
        base_ref[child, mine] += own_ref[child]


def downward(source, offset, x, mate, first, last, own, sigma, radiate, one, two, table, incoming):
    octants, k2, k1 = two.shape
    count, u, r = x.shape
    parents, width = source.shape
    return pl.pallas_call(
        functools.partial(downward_kernel, width),
        out_shape=jax.ShapeDtypeStruct((count, u, r), F32),
        grid_spec=pltpu.PrefetchScalarGridSpec(
            num_scalar_prefetch=2,
            grid=(octants,),
            in_specs=[
                ANY,
                ANY,
                ANY,
                ANY,
                pl.BlockSpec((8, u // 2, r), lambda i, *_: (i, 0, 0)),
                pl.BlockSpec(memory_space=pltpu.SMEM),
                VMEM,
                VMEM,
                VMEM,
                pl.BlockSpec((1, k2, k1), lambda i, *_: (i, 0, 0)),
                VMEM,
                VMEM,
            ],
            out_specs=pl.BlockSpec((8, u, r), lambda i, *_: (i, 0, 0)),
            scratch_shapes=[
                pltpu.VMEM((3 * count, u, r), BF),
                pltpu.VMEM((3 * parents, r, k1), BF),
                pltpu.VMEM((r, k2), BF),
                pltpu.VMEM((width, k1), F32),
                pltpu.VMEM((r, k1), F32),
                pltpu.SemaphoreType.DMA((3,)),
            ],
        ),
        compiler_params=pltpu.CompilerParams(vmem_limit_bytes=40 * MIB),
        cost_estimate=pl.CostEstimate(flops=9_000_000_000, bytes_accessed=60 * MIB, transcendentals=0),
        name="downward",
    )(
        source.reshape(-1), offset.reshape(-1), x, mate, first, last, own, sigma.reshape(-1), radiate,
        radiate.T, one, two, table, incoming,
    )


def add_kernel(_, base_ref, back_ref, out_ref):
    out_ref[...] = base_ref[...] + back_ref[...].astype(F32)


def add_rows(base, back, half_at):
    count, u, r = base.shape
    group = 16
    rows = pl.BlockSpec((group, u // 2, r), lambda i, at: (i, at[0], 0))
    return pl.pallas_call(
        add_kernel,
        out_shape=jax.ShapeDtypeStruct((count, u, r), F32),
        grid_spec=pltpu.PrefetchScalarGridSpec(
            num_scalar_prefetch=1,
            grid=(count // group,),
            in_specs=[rows, pl.BlockSpec((group, u // 2, r), lambda i, at: (i, 0, 0))],
            out_specs=rows,
        ),
        input_output_aliases={1: 0},
        compiler_params=pltpu.CompilerParams(vmem_limit_bytes=16 * MIB),
        cost_estimate=pl.CostEstimate(flops=0, bytes_accessed=5 * MIB, transcendentals=0),
        name="add_rows",
    )(half_at, base, back)


def body(
    vectors,
    sigma,
    near_blocks,
    near_index,
    radiate,
    interp_one,
    interp_two,
    trans_one,
    level1_source,
    level1_offset,
    trans_two,
    level2_source,
    level2_offset,
):
    x = vectors[0]
    boxes = lax.axis_size("box")
    k2 = interp_two.shape[1]
    hops = routes(boxes)
    swap = [(i, i ^ 1) for i in range(boxes)]
    first = lax.ppermute(x, BOTH, hops[0])
    mate = lax.ppermute(x, "box", swap)
    partner = lax.ppermute(first, BOTH, hops[1])
    partner_mate = lax.ppermute(partner, "box", swap)
    last = lax.ppermute(partner, BOTH, hops[2])

    coarse = upward(x, radiate, interp_one, interp_two)
    gathered = exchange(coarse.reshape(boxes, k2 // boxes, -1))
    turned = translate(gathered, trans_two, level2_source, level2_offset)
    incoming = exchange(turned).reshape(k2, -1)

    own, other = near_field(near_index, near_blocks, x, mate, first, partner, partner_mate, last)
    back = lax.ppermute(other, "shift", [(0, 1), (1, 0)])
    base = downward(
        level1_source, level1_offset, x, mate, first, last, own, sigma, radiate, interp_one,
        interp_two, trans_one, incoming,
    )
    half_at = (1 - lax.axis_index("shift")).astype(jnp.int32).reshape(1)
    return add_rows(base, back, half_at)[None]


def solution(mesh):
    in_specs = (
        P("shift", "box", None, None),
        P("shift", None),
        P("box", None, "shift", None),
        P("box", None),
        P(),
        P(),
        P(),
        P(),
        P("box", None),
        P("box", None),
        P(None, "box"),
        P(),
        P(),
    )
    out_specs = P("shift", "box", None, None)
    return jax.shard_map(body, mesh=mesh, in_specs=in_specs, out_specs=out_specs, check_vma=False)
```

```python
import functools

import jax
import jax.numpy as jnp
from jax import lax
from jax.experimental import pallas as pl
from jax.experimental.pallas import tpu as pltpu
from jax.sharding import PartitionSpec as P

BF = jnp.bfloat16
F32 = jnp.float32
MIB = 1 << 20
ANY = pl.BlockSpec(memory_space=pl.ANY)
VMEM = pl.BlockSpec(memory_space=pltpu.VMEM)
BOTH = ("box", "shift")
DEPTH = 4


def dot(a, b):
    return jnp.dot(a, b, preferred_element_type=F32)


def dot_nt(a, b):
    return lax.dot_general(a, b, (((1,), (1,)), ((), ())), preferred_element_type=F32)


def routes(boxes):
    chips = boxes // 2

    def flat(chip, core, shift):
        return (chip % chips * 2 + core) * 2 + shift

    hops = ([], [], [])
    for chip in range(chips):
        for core in range(2):
            wraps = chip % DEPTH == (DEPTH - 1 if core else 0)
            beside = chip + (1 if core else -1)
            for shift in range(2):
                stops = [
                    flat(chip, core, shift),
                    flat(beside, 1 - core, 1 - shift if wraps else shift),
                    flat(chip, core, 1 - shift),
                    flat(beside, 1 - core, shift if wraps else 1 - shift),
                ]
                for hop in range(3):
                    hops[hop].append((stops[hop], stops[hop + 1]))
    return hops


def place():
    me = lax.axis_index("box")
    core = lax.rem(me, 2)
    depth = lax.rem(lax.div(me, 2), DEPTH)
    wraps = jnp.where(core == 0, depth == 0, depth == DEPTH - 1).astype(jnp.int32)
    return me, core, wraps


def exchange_kernel(chips, parts, x_ref, *refs):
    sources, refs = refs[:parts], refs[parts:]
    o_ref, refs = refs[0], refs[1:]
    to_mate, refs = refs[:parts], refs[parts:]
    to_neighbour, refs = refs[:parts], refs[parts:]
    held, send, recv, mate_send, mate_recv, local, part_send, part_recv = refs
    me, core, wraps = place()
    shift = lax.axis_index("shift")
    chip = lax.div(me, 2)
    mate = me + 1 - 2 * core
    beside = lax.rem(chip + chips - 1 + 2 * core, chips) * 2 + 1 - core
    beside_shift = shift + wraps * (1 - 2 * shift)
    barrier = pltpu.get_barrier_semaphore()

    def greet(box, along):
        pl.semaphore_signal(
            barrier, inc=1, device_id=(box, along), device_id_type=pl.DeviceIdType.MESH
        )

    greet(mate, shift)
    if parts:
        greet(beside, beside_shift)

    @pl.loop(1, chips)
    def _(step):
        greet(lax.rem(chip + step, chips) * 2 + core, shift)

    own = pltpu.make_async_copy(x_ref.at[:, core], held.at[:, core], local)
    own.start()
    pl.semaphore_wait(barrier, chips + (1 if parts else 0))
    across = pltpu.make_async_remote_copy(
        x_ref.at[:, 1 - core],
        held.at[:, core],
        mate_send,
        mate_recv,
        device_id=(mate, shift),
        device_id_type=pl.DeviceIdType.MESH,
    )
    across.start()
    own.wait()
    across.wait()

    @pl.loop(1, chips)
    def _(step):
        other = lax.rem(chip + step, chips)
        pltpu.make_async_remote_copy(
            held.at[other],
            o_ref.at[chip],
            send,
            recv,
            device_id=(other * 2 + core, shift),
            device_id_type=pl.DeviceIdType.MESH,
        ).start()

    moves = []
    for i in range(parts):
        for j, (ref, device) in enumerate(
            ((to_neighbour[i], (beside, beside_shift)), (to_mate[i], (mate, shift)))
        ):
            move = pltpu.make_async_remote_copy(
                sources[i],
                ref,
                part_send.at[2 * i + j],
                part_recv.at[2 * i + j],
                device_id=device,
                device_id_type=pl.DeviceIdType.MESH,
            )
            move.start()
            moves.append(move)
    own = pltpu.make_async_copy(held.at[chip], o_ref.at[chip], local)
    own.start()
    own.wait()
    rest = pl.ds(0, chips - 1)
    pltpu.make_async_copy(held.at[rest], held.at[rest], send).wait()
    pltpu.make_async_copy(o_ref.at[rest], o_ref.at[rest], recv).wait()
    for move in moves:
        move.wait()


def exchange(blocks, *parts):
    count, samples, r = blocks.shape
    shape = (count // 2, 2, samples, r)
    n = len(parts)
    blocks, *moved = pl.pallas_call(
        functools.partial(exchange_kernel, count // 2, n),
        out_shape=[jax.ShapeDtypeStruct(shape, BF)]
        + [jax.ShapeDtypeStruct(part.shape, BF) for part in parts] * 2,
        in_specs=[VMEM] + [ANY] * n,
        out_specs=[VMEM] + [ANY] * (2 * n),
        scratch_shapes=[pltpu.VMEM(shape, BF)]
        + [pltpu.SemaphoreType.DMA] * 5
        + [pltpu.SemaphoreType.DMA((max(2 * n, 1),))] * 2,
        compiler_params=pltpu.CompilerParams(
            has_side_effects=True, collective_id=1 if n else 0, vmem_limit_bytes=56 * MIB
        ),
        cost_estimate=pl.CostEstimate(flops=0, bytes_accessed=80 * MIB, transcendentals=0),
        name="exchange",
    )(blocks.reshape(shape), *parts)
    return blocks.reshape(count, samples, r), *moved


def identity(n):
    shape = (n, n)
    same = lax.broadcasted_iota(jnp.int32, shape, 0) == lax.broadcasted_iota(jnp.int32, shape, 1)
    return same.astype(BF)


def two_parents(x_of, radiate, one_ref):
    total = None
    for pair in range(4):
        leaves = [
            dot(radiate, jnp.concatenate([x_of(o), x_of(8 + o)], axis=1)).astype(BF)
            for o in (2 * pair, 2 * pair + 1)
        ]
        lhs = jnp.concatenate([one_ref[2 * pair], one_ref[2 * pair + 1]], axis=1)
        term = dot(lhs, jnp.concatenate(leaves, axis=0))
        total = term if total is None else total + term
    return total


def upward_kernel(x_ref, radiate_ref, one_ref, two_ref, coarse_ref, patterns_ref, total):
    step = pl.program_id(0)
    upper = two_parents(lambda i: x_ref[i], radiate_ref[...], one_ref).astype(BF)
    r = x_ref.shape[2]
    left, right = upper[:, :r], upper[:, r:]
    term = dot(two_ref[0], left) + dot(two_ref[1], right)

    @pl.when(step == 0)
    def _():
        total[...] = term

    @pl.when(step > 0)
    def _():
        total[...] += term

    eye = identity(r)
    patterns_ref[0] = dot_nt(eye, left).astype(BF)
    patterns_ref[1] = dot_nt(eye, right).astype(BF)

    @pl.when(step == pl.num_programs(0) - 1)
    def _():
        coarse_ref[...] = total[...].astype(BF)


def upward(x, radiate, one, two):
    octants, k2, k1 = two.shape
    count, u, r = x.shape
    return pl.pallas_call(
        upward_kernel,
        grid=(octants // 2,),
        out_shape=[
            jax.ShapeDtypeStruct((k2, r), BF),
            jax.ShapeDtypeStruct((count // 8, r, k1), BF),
        ],
        in_specs=[
            pl.BlockSpec((16, u, r), lambda i: (i, 0, 0)),
            VMEM,
            VMEM,
            pl.BlockSpec((2, k2, k1), lambda i: (i, 0, 0)),
        ],
        out_specs=[
            pl.BlockSpec((k2, r), lambda i: (0, 0)),
            pl.BlockSpec((2, r, k1), lambda i: (i, 0, 0)),
        ],
        scratch_shapes=[pltpu.VMEM((k2, r), F32)],
        compiler_params=pltpu.CompilerParams(vmem_limit_bytes=56 * MIB),
        cost_estimate=pl.CostEstimate(flops=7_000_000_000, bytes_accessed=50 * MIB, transcendentals=0),
        name="upward",
    )(x, radiate, one, two)


def fill_patterns(x_of, patterns, at, radiate, one_ref):
    for pair in range(2):
        upper = two_parents(lambda i: x_of(16 * pair + i), radiate, one_ref).astype(BF)
        r = upper.shape[1] // 2
        eye = identity(r)
        patterns[at + 2 * pair] = dot_nt(eye, upper[:, :r]).astype(BF)
        patterns[at + 2 * pair + 1] = dot_nt(eye, upper[:, r:]).astype(BF)


def beside_kernel(_, mate_ref, a_ref, b_ref, radiate_ref, one_ref, patterns_ref):
    step = pl.program_id(0)
    for when, ref in ((step < 2, mate_ref), (step == 2, a_ref), (step == 3, b_ref)):

        @pl.when(when)
        def _(ref=ref):
            fill_patterns(lambda i: ref[i], patterns_ref, 0, radiate_ref[...], one_ref)


def patterns_beside(core, mate, first_a, first_b, radiate, one):
    count, u, r = mate.shape
    _, k1, k0 = one.shape

    def where(i, core):
        towards = 4 * core[0]
        return (jnp.where(i < 2, 4 - towards + i, towards + jnp.where(i == 2, 1 - core[0], core[0])), 0, 0)

    whole = pl.BlockSpec((count // 2, u, r), lambda i, _: (0, 0, 0))
    return pl.pallas_call(
        beside_kernel,
        out_shape=jax.ShapeDtypeStruct((3 * count // 8, r, k1), BF),
        grid_spec=pltpu.PrefetchScalarGridSpec(
            num_scalar_prefetch=1,
            grid=(4,),
            in_specs=[
                pl.BlockSpec((count // 2, u, r), lambda i, _: (jnp.minimum(i, 1), 0, 0)),
                whole,
                whole,
                VMEM,
                VMEM,
            ],
            out_specs=pl.BlockSpec((count // 16, r, k1), where),
        ),
        compiler_params=pltpu.CompilerParams(vmem_limit_bytes=56 * MIB),
        cost_estimate=pl.CostEstimate(flops=4_000_000_000, bytes_accessed=30 * MIB, transcendentals=0),
        name="patterns_beside",
    )(core, mate, first_a, first_b, radiate, one)


def translate_kernel(width, source_ref, offset_ref, rounds_ref, coarse_ref, weight_ref, out_ref):
    @pl.loop(0, out_ref.shape[0])
    def _(box):
        def four(step, total):
            for j in range(4):
                at = box * width + step * 4 + j
                total += weight_ref[offset_ref[at]] * coarse_ref[source_ref[at]].astype(F32)
            return total

        start = jnp.zeros(out_ref.shape[1:], F32)
        out_ref[box] = lax.fori_loop(0, rounds_ref[box], four, start).astype(BF)


def translation_lists(table, source, offset, columns):
    classes, samples = table.shape
    live = source >= 0
    rounds = (jnp.sum(live.astype(jnp.int32), axis=1) + 3) // 4
    weights = jnp.broadcast_to(
        jnp.pad(table, ((0, 1), (0, 0)))[:, :, None], (classes + 1, samples, columns)
    )
    return (
        jnp.where(live, source, 0).reshape(-1),
        jnp.where(live, offset, classes).reshape(-1),
        rounds,
        weights,
    )


def translate(coarse, source, offset, rounds, weights):
    return pl.pallas_call(
        functools.partial(translate_kernel, source.shape[0] // coarse.shape[0]),
        out_shape=jax.ShapeDtypeStruct(coarse.shape, BF),
        grid_spec=pltpu.PrefetchScalarGridSpec(
            num_scalar_prefetch=3, grid=(), in_specs=[VMEM, VMEM], out_specs=VMEM
        ),
        compiler_params=pltpu.CompilerParams(vmem_limit_bytes=16 * MIB),
        cost_estimate=pl.CostEstimate(flops=2_000_000_000, bytes_accessed=25 * MIB, transcendentals=0),
        name="translate",
    )(source, offset, rounds, coarse, weights)


def near_kernel(group, slots, part, index_ref, halves_ref, blocks_ref, *refs):
    sources, (own_ref, other_ref, held, sems) = refs[:-4], refs[-4:]
    step = pl.program_id(0)
    me, core, wraps = place()
    count = sources[0].shape[0]
    half = count // 2

    @pl.when(step == 0)
    def _():
        towards = 2 * core * count
        within = 2 * count - towards
        upper, lower = half * (1 - core), half * core
        places = (
            (0, count),
            (0, within),
            (1, count + lower),
            (1, count + upper),
            (1, within + upper),
            (1, within + lower),
            (wraps, towards + upper),
            (1 - wraps, towards + upper),
            (wraps, towards + lower),
            (1 - wraps, towards + lower),
        )
        copies = [
            pltpu.make_async_copy(src, held.at[kind, pl.ds(at, src.shape[0])], sems.at[i])
            for i, (src, (kind, at)) in enumerate(zip(sources, places))
        ]
        for copy in copies:
            copy.start()
        zero = jnp.zeros(held.shape[2:], BF)
        held[0, 3 * count] = zero
        held[1, 3 * count] = zero
        for copy in copies:
            copy.wait()

    base = me * count - count
    origin = halves_ref[part] * half + step * group
    for b in range(group):
        total = None
        for pair in range(slots // 2):
            rows = []
            for i in range(2):
                at = index_ref[(origin + b) * slots + 2 * pair + i]
                at = jnp.where(at >= 0, at - base, 3 * count)
                rows.append(jnp.concatenate([held[0, at], held[1, at]], axis=1))
            lhs = jnp.concatenate([blocks_ref[b, 2 * pair], blocks_ref[b, 2 * pair + 1]], axis=1)
            term = dot(lhs, jnp.concatenate(rows, axis=0))
            total = term if total is None else total + term
        r = own_ref.shape[2]
        own_ref[b] = total[:, :r]
        other_ref[b] = total[:, r:].astype(BF)


def near_field(part, halves, index, blocks, *sources):
    count, slots, rows, u = blocks.shape
    r = sources[0].shape[2]
    group = 8
    steps = count // 2 // group
    out = pl.BlockSpec((group, rows, r), lambda i, *_: (i, 0, 0))
    return pl.pallas_call(
        functools.partial(near_kernel, group, slots, part),
        out_shape=[
            jax.ShapeDtypeStruct((count // 2, rows, r), F32),
            jax.ShapeDtypeStruct((count // 2, rows, r), BF),
        ],
        grid_spec=pltpu.PrefetchScalarGridSpec(
            num_scalar_prefetch=2,
            grid=(steps,),
            in_specs=[
                pl.BlockSpec((group, slots, rows, u), lambda i, _, h: (h[part] * steps + i, 0, 0, 0))
            ]
            + [ANY] * len(sources),
            out_specs=[out, out],
            scratch_shapes=[
                pltpu.VMEM((2, 3 * count + 1, u, r), BF),
                pltpu.SemaphoreType.DMA((len(sources),)),
            ],
        ),
        compiler_params=pltpu.CompilerParams(vmem_limit_bytes=56 * MIB),
        cost_estimate=pl.CostEstimate(flops=3_000_000_000, bytes_accessed=20 * MIB, transcendentals=0),
        name="near_field",
    )(index, halves, blocks, *sources)


def local_step(
    width, step, source_ref, offset_ref, last_a, last_b, mine, beside, radiate_ref, one_ref, two_ref,
    table_ref, incoming_ref, held, patterns, flat, weights, across, local, sems,
):
    me, core, wraps = place()
    count, u, r = held.shape
    parents = count // 8
    half = count // 2

    @pl.when(step == 0)
    def _():
        towards = 2 * core * parents
        within = pl.ds(2 * parents - towards, parents)
        center = pl.ds(parents, parents)
        copies = [
            pltpu.make_async_copy(mine, patterns.at[center], sems.at[0]),
            pltpu.make_async_copy(beside.at[within], patterns.at[within], sems.at[1]),
        ]
        for copy in copies:
            copy.start()
        flat[...] = dot_nt(identity(r), incoming_ref[...]).astype(BF)

        @pl.when(wraps == 0)
        def _():
            there = pl.ds(towards, parents)
            copy = pltpu.make_async_copy(beside.at[there], patterns.at[there], sems.at[2])
            copy.start()
            copy.wait()

        @pl.when(wraps == 1)
        def _():
            halves = [
                pltpu.make_async_copy(last_a, held.at[pl.ds(half * (1 - core), half)], sems.at[2]),
                pltpu.make_async_copy(last_b, held.at[pl.ds(half * core, half)], sems.at[3]),
            ]
            for copy in halves:
                copy.start()
            for copy in halves:
                copy.wait()

            @pl.loop(0, 2)
            def _(i):
                fill_patterns(
                    lambda k: held[i * half + k], patterns, towards + i * 4, radiate_ref[...], one_ref
                )

        for copy in copies:
            copy.wait()

    origin = me * parents - parents
    at = []
    for j in range(width):
        source = source_ref[step * width + j]
        live = source >= 0
        at.append(jnp.where(live, source - origin, parents))
        row = table_ref[pl.ds(offset_ref[step * width + j], 1), :]
        weights[pl.ds(j, 1), :] = row * live.astype(F32)

    @pl.loop(0, r // 16)
    def _(part):
        rows = pl.ds(pl.multiple_of(part * 16, 16), 16)
        total = None
        for j in range(width):
            term = weights[pl.ds(j, 1), :] * patterns[at[j], rows, :].astype(F32)
            total = term if total is None else total + term
        across[rows, :] = total

    local[pl.ds(pl.multiple_of(step * r, r), r), :] = (
        across[...] + dot(flat[...], two_ref[0])
    ).astype(BF)


def downward_kernel(
    width, source_ref, offset_ref, x_ref, last_a, last_b, mine, beside, a_ref, b_ref, sigma_ref,
    radiate_ref, turned_ref, one_ref, two_ref, table_ref, incoming_ref, base_ref,
    held, patterns, flat, weights, across, local, sems,
):
    step = pl.program_id(0)
    parents, _, u, r = x_ref.shape
    rows = u // 2

    @pl.when(step < parents)
    def _():
        local_step(
            width, step, source_ref, offset_ref, last_a, last_b, mine, beside, radiate_ref, one_ref,
            two_ref, table_ref, incoming_ref, held, patterns, flat, weights, across, local, sems,
        )

    @pl.when(step >= parents)
    def _():
        core = lax.rem(lax.axis_index("box"), 2)
        own = pl.ds(pl.multiple_of(lax.axis_index("shift") * rows, rows), rows)
        sig_re, sig_im = sigma_ref[0], sigma_ref[1]
        leaf_in = dot(local[...], one_ref[step - parents]).astype(BF)
        far = dot_nt(turned_ref[...], leaf_in)
        for c in range(parents):
            part = far[:, c * r : (c + 1) * r]
            field = x_ref[c, 0].astype(F32)
            real, imag = field[:rows], field[rows:]
            base_ref[c, 0, :rows] = part[:rows] - (sig_re * real - sig_im * imag)
            base_ref[c, 0, rows:] = part[rows:] - (sig_re * imag + sig_im * real)
            at = c % (parents // 2)
            in_a = core == (1 if c < parents // 2 else 0)
            base_ref[c, 0, own] += jnp.where(in_a, a_ref[at, 0], b_ref[at, 0])


def downward(
    source, offset, x, last_a, last_b, mine, beside, own_a, own_b, sigma, radiate, turned, one, two,
    table, incoming,
):
    octants, k2, k1 = two.shape
    count, u, r = x.shape
    parents = count // 8
    width = source.shape[0] // parents

    def child(i, *_):
        return (0, jnp.maximum(i - parents, 0), 0, 0)

    near = pl.BlockSpec((parents // 2, 1, u // 2, r), child)
    box = pl.BlockSpec((parents, 1, u, r), child)
    return pl.pallas_call(
        functools.partial(downward_kernel, width),
        out_shape=jax.ShapeDtypeStruct((parents, 8, u, r), F32),
        grid_spec=pltpu.PrefetchScalarGridSpec(
            num_scalar_prefetch=2,
            grid=(parents + 8,),
            in_specs=[
                box,
                ANY,
                ANY,
                ANY,
                ANY,
                near,
                near,
                pl.BlockSpec(memory_space=pltpu.SMEM),
                VMEM,
                VMEM,
                VMEM,
                pl.BlockSpec((1, k2, k1), lambda i, *_: (jnp.minimum(i, parents - 1), 0, 0)),
                VMEM,
                VMEM,
            ],
            out_specs=box,
            scratch_shapes=[
                pltpu.VMEM((count, u, r), BF),
                pltpu.VMEM((3 * parents, r, k1), BF),
                pltpu.VMEM((r, k2), BF),
                pltpu.VMEM((width, k1), F32),
                pltpu.VMEM((r, k1), F32),
                pltpu.VMEM((parents * r, k1), BF),
                pltpu.SemaphoreType.DMA((4,)),
            ],
        ),
        compiler_params=pltpu.CompilerParams(vmem_limit_bytes=56 * MIB),
        cost_estimate=pl.CostEstimate(flops=9_000_000_000, bytes_accessed=80 * MIB, transcendentals=0),
        name="downward",
    )(
        source, offset, x.reshape(parents, 8, u, r), last_a, last_b, mine, beside,
        own_a.reshape(parents // 2, 8, u // 2, r), own_b.reshape(parents // 2, 8, u // 2, r),
        sigma.reshape(-1), radiate, turned, one, two, table, incoming,
    ).reshape(count, u, r)


def add_kernel(_, base_ref, back_ref, out_ref):
    out_ref[...] = base_ref[...] + back_ref[...].astype(F32)


def add_rows(where, base, back):
    count, u, r = base.shape
    group = count // 4
    rows = pl.BlockSpec((group, u // 2, r), lambda i, at: (at[0] * 2 + i, at[1], 0))
    return pl.pallas_call(
        add_kernel,
        out_shape=jax.ShapeDtypeStruct((count, u, r), F32),
        grid_spec=pltpu.PrefetchScalarGridSpec(
            num_scalar_prefetch=1,
            grid=(2,),
            in_specs=[rows, pl.BlockSpec((group, u // 2, r), lambda i, at: (i, 0, 0))],
            out_specs=rows,
        ),
        input_output_aliases={1: 0},
        compiler_params=pltpu.CompilerParams(vmem_limit_bytes=16 * MIB),
        cost_estimate=pl.CostEstimate(flops=0, bytes_accessed=3 * MIB, transcendentals=0),
        name="add_rows",
    )(where, base, back)


def after(arrays, *others):
    return lax.optimization_barrier((tuple(arrays), others))[0]


def body(
    vectors,
    sigma,
    near_blocks,
    near_index,
    radiate,
    interp_one,
    interp_two,
    trans_one,
    level1_source,
    level1_offset,
    trans_two,
    level2_source,
    level2_offset,
):
    x = vectors[0]
    count = x.shape[0]
    boxes = lax.axis_size("box")
    k2 = interp_two.shape[1]
    hops = routes(boxes)
    swap = [(i, i ^ 1) for i in range(boxes)]
    partners = [(0, 1), (1, 0)]
    core = lax.rem(lax.axis_index("box"), 2).astype(jnp.int32)
    shift = lax.axis_index("shift").astype(jnp.int32)
    halves = jnp.stack([1 - core, core])
    lists = (
        near_index.reshape(-1),
        level1_source.reshape(-1),
        level1_offset.reshape(-1),
        radiate.T,
        halves,
        jnp.stack([1 - core, 1 - shift]),
        jnp.stack([core, 1 - shift]),
        *translation_lists(trans_two, level2_source, level2_offset, x.shape[2]),
    )

    first_a, first_b = [
        lax.ppermute(lax.dynamic_slice_in_dim(x, at * (count // 2), count // 2), BOTH, hops[0])
        for at in (core, 1 - core)
    ]
    mate = lax.ppermute(x, "box", swap)
    coarse, mine = upward(x, radiate, interp_one, interp_two)

    (first_a,) = after([first_a], coarse)
    partner_a = lax.ppermute(first_a, BOTH, hops[1])
    coarse, *lists = after([coarse, *lists], first_a)
    index, source, offset, turned_radiate, halves, where_a, where_b, *translation = lists
    (gathered,) = exchange(coarse.reshape(boxes, k2 // boxes, -1))

    first_b, partner_a = after([first_b, partner_a], gathered)
    partner_b = lax.ppermute(first_b, BOTH, hops[1])
    turned = translate(gathered, *translation)
    beside = patterns_beside(core.reshape(1), mate, first_a, first_b, radiate, interp_one)
    (turned,) = after([turned], beside)
    incoming, partner_mate_a, partner_mate_b, last_a, last_b = exchange(turned, partner_a, partner_b)
    incoming = incoming.reshape(k2, -1)
    (index,) = after([index], incoming)
    here = (x, mate, partner_a, partner_b, partner_mate_a, partner_mate_b, first_a, last_a)
    own_a, other_a = near_field(0, halves, index, near_blocks, *here)
    back_a = lax.ppermute(other_a, "shift", partners)
    (index,) = after([index], other_a)
    own_b, other_b = near_field(1, halves, index, near_blocks, *here, first_b, last_b)
    back_b = lax.ppermute(other_b, "shift", partners)
    base = downward(
        source, offset, x, last_a, last_b, mine, beside, own_a, own_b, sigma, radiate, turned_radiate,
        interp_one, interp_two, trans_one, incoming,
    )
    base = add_rows(where_a, base, back_a)
    return add_rows(where_b, base, back_b)[None]


def solution(mesh):
    in_specs = (
        P("shift", "box", None, None),
        P("shift", None),
        P("box", None, "shift", None),
        P("box", None),
        P(),
        P(),
        P(),
        P(),
        P("box", None),
        P("box", None),
        P(None, "box"),
        P(),
        P(),
    )
    out_specs = P("shift", "box", None, None)
    return jax.shard_map(body, mesh=mesh, in_specs=in_specs, out_specs=out_specs, check_vma=False)
```

```python
import functools

import jax
import jax.numpy as jnp
from jax import lax
from jax.experimental import pallas as pl
from jax.experimental.pallas import tpu as pltpu
from jax.sharding import PartitionSpec as P

BF = jnp.bfloat16
F32 = jnp.float32
MIB = 1 << 20
ANY = pl.BlockSpec(memory_space=pl.ANY)
VMEM = pl.BlockSpec(memory_space=pltpu.VMEM)
BOTH = ("box", "shift")
DEPTH = 4


def dot(a, b):
    return jnp.dot(a, b, preferred_element_type=F32)


def dot_nt(a, b):
    return lax.dot_general(a, b, (((1,), (1,)), ((), ())), preferred_element_type=F32)


def routes(boxes):
    chips = boxes // 2

    def flat(chip, core, shift):
        return (chip % chips * 2 + core) * 2 + shift

    hops = ([], [], [])
    for chip in range(chips):
        for core in range(2):
            wraps = chip % DEPTH == (DEPTH - 1 if core else 0)
            beside = chip + (1 if core else -1)
            for shift in range(2):
                stops = [
                    flat(chip, core, shift),
                    flat(beside, 1 - core, 1 - shift if wraps else shift),
                    flat(chip, core, 1 - shift),
                    flat(beside, 1 - core, shift if wraps else 1 - shift),
                ]
                for hop in range(3):
                    hops[hop].append((stops[hop], stops[hop + 1]))
    return hops


def place():
    me = lax.axis_index("box")
    core = lax.rem(me, 2)
    depth = lax.rem(lax.div(me, 2), DEPTH)
    wraps = jnp.where(core == 0, depth == 0, depth == DEPTH - 1).astype(jnp.int32)
    return me, core, wraps


def exchange_kernel(chips, parts, x_ref, *refs):
    sources, refs = refs[:parts], refs[parts:]
    o_ref, refs = refs[0], refs[1:]
    targets, refs = refs[: parts + 1 if parts else 0], refs[parts + 1 if parts else 0 :]
    held, send, recv, mate_send, mate_recv, local, part_send, part_recv = refs
    me, core, wraps = place()
    shift = lax.axis_index("shift")
    chip = lax.div(me, 2)
    mate = me + 1 - 2 * core
    beside = lax.rem(chip + chips - 1 + 2 * core, chips) * 2 + 1 - core
    beside_shift = shift + wraps * (1 - 2 * shift)
    barrier = pltpu.get_barrier_semaphore()

    def greet(box, along):
        pl.semaphore_signal(
            barrier, inc=1, device_id=(box, along), device_id_type=pl.DeviceIdType.MESH
        )

    if parts:
        greet(beside, beside_shift)
    greet(mate, shift)

    @pl.loop(1, chips)
    def _(step):
        greet(lax.rem(chip + step, chips) * 2 + core, shift)

    own = pltpu.make_async_copy(x_ref.at[:, core], held.at[:, core], local)
    own.start()
    pl.semaphore_wait(barrier, chips + (1 if parts else 0))
    across = pltpu.make_async_remote_copy(
        x_ref.at[:, 1 - core],
        held.at[:, core],
        mate_send,
        mate_recv,
        device_id=(mate, shift),
        device_id_type=pl.DeviceIdType.MESH,
    )
    across.start()
    moves = []
    if parts:
        ends = [(source, (mate, shift)) for source in sources]
        ends.append((sources[-1], (beside, beside_shift)))
        for i in reversed(range(parts + 1)):
            move = pltpu.make_async_remote_copy(
                ends[i][0],
                targets[i],
                part_send.at[i],
                part_recv.at[i],
                device_id=ends[i][1],
                device_id_type=pl.DeviceIdType.MESH,
            )
            move.start()
            moves.append(move)
    own.wait()
    across.wait()

    @pl.loop(1, chips)
    def _(step):
        other = lax.rem(chip + step, chips)
        pltpu.make_async_remote_copy(
            held.at[other],
            o_ref.at[chip],
            send,
            recv,
            device_id=(other * 2 + core, shift),
            device_id_type=pl.DeviceIdType.MESH,
        ).start()

    own = pltpu.make_async_copy(held.at[chip], o_ref.at[chip], local)
    own.start()
    own.wait()
    rest = pl.ds(0, chips - 1)
    pltpu.make_async_copy(held.at[rest], held.at[rest], send).wait()
    pltpu.make_async_copy(o_ref.at[rest], o_ref.at[rest], recv).wait()
    for move in moves:
        move.wait()


def exchange(blocks, *parts):
    count, samples, r = blocks.shape
    shape = (count // 2, 2, samples, r)
    moved = [*parts, *parts[-1:]]
    n = len(parts)
    blocks, *moved = pl.pallas_call(
        functools.partial(exchange_kernel, count // 2, n),
        out_shape=[jax.ShapeDtypeStruct(shape, BF)]
        + [jax.ShapeDtypeStruct(part.shape, BF) for part in moved],
        in_specs=[VMEM] + [ANY] * n,
        out_specs=[VMEM] + [ANY] * len(moved),
        scratch_shapes=[pltpu.VMEM(shape, BF)]
        + [pltpu.SemaphoreType.DMA] * 5
        + [pltpu.SemaphoreType.DMA((max(len(moved), 1),))] * 2,
        compiler_params=pltpu.CompilerParams(
            has_side_effects=True, collective_id=1 if n else 0, vmem_limit_bytes=56 * MIB
        ),
        cost_estimate=pl.CostEstimate(flops=0, bytes_accessed=80 * MIB, transcendentals=0),
        name="exchange",
    )(blocks.reshape(shape), *parts)
    return blocks.reshape(count, samples, r), *moved


def identity(n):
    shape = (n, n)
    same = lax.broadcasted_iota(jnp.int32, shape, 0) == lax.broadcasted_iota(jnp.int32, shape, 1)
    return same.astype(BF)


def two_parents(x_of, radiate, one_ref):
    total = None
    for pair in range(4):
        leaves = [
            dot(radiate, jnp.concatenate([x_of(o), x_of(8 + o)], axis=1)).astype(BF)
            for o in (2 * pair, 2 * pair + 1)
        ]
        lhs = jnp.concatenate([one_ref[2 * pair], one_ref[2 * pair + 1]], axis=1)
        term = dot(lhs, jnp.concatenate(leaves, axis=0))
        total = term if total is None else total + term
    return total


def upward_kernel(x_ref, radiate_ref, one_ref, two_ref, coarse_ref, patterns_ref, total):
    step = pl.program_id(0)
    upper = two_parents(lambda i: x_ref[i], radiate_ref[...], one_ref).astype(BF)
    r = x_ref.shape[2]
    left, right = upper[:, :r], upper[:, r:]
    term = dot(two_ref[0], left) + dot(two_ref[1], right)

    @pl.when(step == 0)
    def _():
        total[...] = term

    @pl.when(step > 0)
    def _():
        total[...] += term

    eye = identity(r)
    patterns_ref[0] = dot_nt(eye, left).astype(BF)
    patterns_ref[1] = dot_nt(eye, right).astype(BF)

    @pl.when(step == pl.num_programs(0) - 1)
    def _():
        coarse_ref[...] = total[...].astype(BF)


def upward(x, radiate, one, two):
    octants, k2, k1 = two.shape
    count, u, r = x.shape
    return pl.pallas_call(
        upward_kernel,
        grid=(octants // 2,),
        out_shape=[
            jax.ShapeDtypeStruct((k2, r), BF),
            jax.ShapeDtypeStruct((count // 8, r, k1), BF),
        ],
        in_specs=[
            pl.BlockSpec((16, u, r), lambda i: (i, 0, 0)),
            VMEM,
            VMEM,
            pl.BlockSpec((2, k2, k1), lambda i: (i, 0, 0)),
        ],
        out_specs=[
            pl.BlockSpec((k2, r), lambda i: (0, 0)),
            pl.BlockSpec((2, r, k1), lambda i: (i, 0, 0)),
        ],
        scratch_shapes=[pltpu.VMEM((k2, r), F32)],
        compiler_params=pltpu.CompilerParams(vmem_limit_bytes=56 * MIB),
        cost_estimate=pl.CostEstimate(flops=7_000_000_000, bytes_accessed=50 * MIB, transcendentals=0),
        name="upward",
    )(x, radiate, one, two)


def fill_patterns(x_of, patterns, at, radiate, one_ref):
    for pair in range(2):
        upper = two_parents(lambda i: x_of(16 * pair + i), radiate, one_ref).astype(BF)
        r = upper.shape[1] // 2
        eye = identity(r)
        patterns[at + 2 * pair] = dot_nt(eye, upper[:, :r]).astype(BF)
        patterns[at + 2 * pair + 1] = dot_nt(eye, upper[:, r:]).astype(BF)


def beside_kernel(_, mate_ref, a_ref, b_ref, radiate_ref, one_ref, patterns_ref):
    step = pl.program_id(0)
    for when, ref in ((step < 2, mate_ref), (step == 2, a_ref), (step == 3, b_ref)):

        @pl.when(when)
        def _(ref=ref):
            fill_patterns(lambda i: ref[i], patterns_ref, 0, radiate_ref[...], one_ref)


def patterns_beside(core, mate, first_a, first_b, radiate, one):
    count, u, r = mate.shape
    _, k1, k0 = one.shape

    def where(i, core):
        towards = 4 * core[0]
        return (jnp.where(i < 2, 4 - towards + i, towards + i - 2), 0, 0)

    whole = pl.BlockSpec((count // 2, u, r), lambda i, _: (0, 0, 0))
    return pl.pallas_call(
        beside_kernel,
        out_shape=jax.ShapeDtypeStruct((3 * count // 8, r, k1), BF),
        grid_spec=pltpu.PrefetchScalarGridSpec(
            num_scalar_prefetch=1,
            grid=(4,),
            in_specs=[
                pl.BlockSpec((count // 2, u, r), lambda i, _: (jnp.minimum(i, 1), 0, 0)),
                whole,
                whole,
                VMEM,
                VMEM,
            ],
            out_specs=pl.BlockSpec((count // 16, r, k1), where),
        ),
        compiler_params=pltpu.CompilerParams(vmem_limit_bytes=56 * MIB),
        cost_estimate=pl.CostEstimate(flops=4_000_000_000, bytes_accessed=30 * MIB, transcendentals=0),
        name="patterns_beside",
    )(core, mate, first_a, first_b, radiate, one)


def translate_kernel(width, source_ref, offset_ref, rounds_ref, coarse_ref, weight_ref, out_ref):
    @pl.loop(0, out_ref.shape[0])
    def _(box):
        def four(step, total):
            for j in range(4):
                at = box * width + step * 4 + j
                total += weight_ref[offset_ref[at]] * coarse_ref[source_ref[at]].astype(F32)
            return total

        start = jnp.zeros(out_ref.shape[1:], F32)
        out_ref[box] = lax.fori_loop(0, rounds_ref[box], four, start).astype(BF)


def translation_lists(table, source, offset, columns):
    classes, samples = table.shape
    live = source >= 0
    rounds = (jnp.sum(live.astype(jnp.int32), axis=1) + 3) // 4
    weights = jnp.broadcast_to(
        jnp.pad(table, ((0, 1), (0, 0)))[:, :, None], (classes + 1, samples, columns)
    )
    return (
        jnp.where(live, source, 0).reshape(-1),
        jnp.where(live, offset, classes).reshape(-1),
        rounds,
        weights,
    )


def translate(coarse, source, offset, rounds, weights):
    return pl.pallas_call(
        functools.partial(translate_kernel, source.shape[0] // coarse.shape[0]),
        out_shape=jax.ShapeDtypeStruct(coarse.shape, BF),
        grid_spec=pltpu.PrefetchScalarGridSpec(
            num_scalar_prefetch=3, grid=(), in_specs=[VMEM, VMEM], out_specs=VMEM
        ),
        compiler_params=pltpu.CompilerParams(vmem_limit_bytes=16 * MIB),
        cost_estimate=pl.CostEstimate(flops=2_000_000_000, bytes_accessed=25 * MIB, transcendentals=0),
        name="translate",
    )(source, offset, rounds, coarse, weights)


def near_kernel(group, slots, start, index_ref, blocks_ref, *refs):
    sources, (own_ref, other_ref, held, sems) = refs[:-4], refs[-4:]
    step = pl.program_id(0)
    me, core, wraps = place()
    count = sources[0].shape[0]
    half = count // 2

    @pl.when(step == 0)
    def _():
        towards = 2 * core * count
        within = 2 * count - towards
        places = (
            (0, count),
            (0, within),
            (1, count),
            (1, count + half),
            (1, within),
            (1, within + half),
            (wraps, towards),
            (wraps, towards + half),
            (1 - wraps, towards),
            (1 - wraps, towards + half),
        )
        copies = [
            pltpu.make_async_copy(src, held.at[kind, pl.ds(at, src.shape[0])], sems.at[i])
            for i, (src, (kind, at)) in enumerate(zip(sources, places))
        ]
        for copy in copies:
            copy.start()
        zero = jnp.zeros(held.shape[2:], BF)
        held[0, 3 * count] = zero
        held[1, 3 * count] = zero
        for copy in copies:
            copy.wait()

    base = me * count - count
    origin = start + step * group
    for b in range(group):
        total = None
        for pair in range(slots // 2):
            rows = []
            for i in range(2):
                at = index_ref[(origin + b) * slots + 2 * pair + i]
                at = jnp.where(at >= 0, at - base, 3 * count)
                rows.append(jnp.concatenate([held[0, at], held[1, at]], axis=1))
            lhs = jnp.concatenate([blocks_ref[b, 2 * pair], blocks_ref[b, 2 * pair + 1]], axis=1)
            term = dot(lhs, jnp.concatenate(rows, axis=0))
            total = term if total is None else total + term
        r = own_ref.shape[2]
        own_ref[b] = total[:, :r]
        other_ref[b] = total[:, r:].astype(BF)


def near_field(start, stop, index, blocks, *sources):
    count, slots, rows, u = blocks.shape
    r = sources[0].shape[2]
    group = 8
    out = pl.BlockSpec((group, rows, r), lambda i, *_: (i, 0, 0))
    return pl.pallas_call(
        functools.partial(near_kernel, group, slots, start),
        out_shape=[
            jax.ShapeDtypeStruct((stop - start, rows, r), F32),
            jax.ShapeDtypeStruct((stop - start, rows, r), BF),
        ],
        grid_spec=pltpu.PrefetchScalarGridSpec(
            num_scalar_prefetch=1,
            grid=((stop - start) // group,),
            in_specs=[
                pl.BlockSpec((group, slots, rows, u), lambda i, _: (start // group + i, 0, 0, 0))
            ]
            + [ANY] * len(sources),
            out_specs=[out, out],
            scratch_shapes=[
                pltpu.VMEM((2, 3 * count + 1, u, r), BF),
                pltpu.SemaphoreType.DMA((len(sources),)),
            ],
        ),
        compiler_params=pltpu.CompilerParams(vmem_limit_bytes=56 * MIB),
        cost_estimate=pl.CostEstimate(flops=3_000_000_000, bytes_accessed=20 * MIB, transcendentals=0),
        name="near_field",
    )(index, blocks, *sources)


def local_kernel(
    width, source_ref, offset_ref, last_a, last_b, mine, beside, radiate_ref, one_ref, two_ref,
    table_ref, incoming_ref, local_ref, held, patterns, flat, weights, across, sems,
):
    step = pl.program_id(0)
    me, core, wraps = place()
    count, u, r = held.shape
    parents = count // 8
    half = count // 2

    @pl.when(step == 0)
    def _():
        towards = 2 * core * parents
        within = pl.ds(2 * parents - towards, parents)
        center = pl.ds(parents, parents)
        copies = [
            pltpu.make_async_copy(mine, patterns.at[center], sems.at[0]),
            pltpu.make_async_copy(beside.at[within], patterns.at[within], sems.at[1]),
        ]
        for copy in copies:
            copy.start()
        flat[...] = dot_nt(identity(r), incoming_ref[...]).astype(BF)

        @pl.when(wraps == 0)
        def _():
            there = pl.ds(towards, parents)
            copy = pltpu.make_async_copy(beside.at[there], patterns.at[there], sems.at[2])
            copy.start()
            copy.wait()

        @pl.when(wraps == 1)
        def _():
            halves = [
                pltpu.make_async_copy(last_a, held.at[pl.ds(0, half)], sems.at[2]),
                pltpu.make_async_copy(last_b, held.at[pl.ds(half, half)], sems.at[3]),
            ]
            for copy in halves:
                copy.start()
            for copy in halves:
                copy.wait()

            @pl.loop(0, 2)
            def _(i):
                fill_patterns(
                    lambda k: held[i * half + k], patterns, towards + i * 4, radiate_ref[...], one_ref
                )

        for copy in copies:
            copy.wait()

    origin = me * parents - parents
    at = []
    for j in range(width):
        source = source_ref[step * width + j]
        live = source >= 0
        at.append(jnp.where(live, source - origin, parents))
        row = table_ref[pl.ds(offset_ref[step * width + j], 1), :]
        weights[pl.ds(j, 1), :] = row * live.astype(F32)

    @pl.loop(0, r // 16)
    def _(part):
        rows = pl.ds(pl.multiple_of(part * 16, 16), 16)
        total = None
        for j in range(width):
            term = weights[pl.ds(j, 1), :] * patterns[at[j], rows, :].astype(F32)
            total = term if total is None else total + term
        across[rows, :] = total

    local_ref[...] = (across[...] + dot(flat[...], two_ref[0])).astype(BF)


def local_field(source, offset, last_a, last_b, mine, beside, radiate, one, two, table, incoming):
    octants, k2, k1 = two.shape
    _, u, r = last_a.shape
    width = source.shape[0] // octants
    return pl.pallas_call(
        functools.partial(local_kernel, width),
        out_shape=jax.ShapeDtypeStruct((octants * r, k1), BF),
        grid_spec=pltpu.PrefetchScalarGridSpec(
            num_scalar_prefetch=2,
            grid=(octants,),
            in_specs=[ANY] * 4
            + [VMEM, VMEM, pl.BlockSpec((1, k2, k1), lambda i, *_: (i, 0, 0)), VMEM, VMEM],
            out_specs=pl.BlockSpec((r, k1), lambda i, *_: (i, 0)),
            scratch_shapes=[
                pltpu.VMEM((octants * 8, u, r), BF),
                pltpu.VMEM((3 * octants, r, k1), BF),
                pltpu.VMEM((r, k2), BF),
                pltpu.VMEM((width, k1), F32),
                pltpu.VMEM((r, k1), F32),
                pltpu.SemaphoreType.DMA((4,)),
            ],
        ),
        compiler_params=pltpu.CompilerParams(vmem_limit_bytes=56 * MIB),
        cost_estimate=pl.CostEstimate(flops=5_000_000_000, bytes_accessed=50 * MIB, transcendentals=0),
        name="local_field",
    )(source, offset, last_a, last_b, mine, beside, radiate, one, two, table, incoming)


def leaves_kernel(
    early, x_ref, a_ref, b_ref, sigma_ref, turned_ref, one_ref, local_ref, base_ref
):
    parents, _, u, r = x_ref.shape
    rows = u // 2
    shift = lax.axis_index("shift")
    own = pl.ds(pl.multiple_of(shift * rows, rows), rows)
    sig_re, sig_im = sigma_ref[0], sigma_ref[1]
    leaf_in = dot(local_ref[...], one_ref[0]).astype(BF)
    far = dot_nt(turned_ref[...], leaf_in)
    for c in range(parents):
        part = far[:, c * r : (c + 1) * r]
        field = x_ref[c, 0].astype(F32)
        real, imag = field[:rows], field[rows:]
        base_ref[c, 0, :rows] = part[:rows] - (sig_re * real - sig_im * imag)
        base_ref[c, 0, rows:] = part[rows:] - (sig_re * imag + sig_im * real)
        base_ref[c, 0, own] += a_ref[c, 0] if c < early else b_ref[c - early, 0]


def leaf_fields(x, own_a, own_b, sigma, turned, one, local):
    count, u, r = x.shape
    octants, k1, k0 = one.shape
    parents = count // octants
    early = own_a.shape[0] // octants

    def apart(array):
        return array.reshape(array.shape[0] // octants, octants, *array.shape[1:])

    def spec(array):
        return pl.BlockSpec((array.shape[0], 1, *array.shape[2:]), lambda i: (0, i, 0, 0))

    parts = [apart(array) for array in (x, own_a, own_b)]
    return pl.pallas_call(
        functools.partial(leaves_kernel, early),
        grid=(octants,),
        out_shape=jax.ShapeDtypeStruct((parents, octants, u, r), F32),
        in_specs=[spec(part) for part in parts]
        + [
            pl.BlockSpec(memory_space=pltpu.SMEM),
            VMEM,
            pl.BlockSpec((1, k1, k0), lambda i: (i, 0, 0)),
            VMEM,
        ],
        out_specs=spec(parts[0]),
        compiler_params=pltpu.CompilerParams(vmem_limit_bytes=56 * MIB),
        cost_estimate=pl.CostEstimate(flops=2_000_000_000, bytes_accessed=20 * MIB, transcendentals=0),
        name="leaf_fields",
    )(*parts, sigma.reshape(-1), turned, one, local).reshape(count, u, r)


def add_kernel(_, base_ref, back_ref, out_ref):
    out_ref[...] = base_ref[...] + back_ref[...].astype(F32)


def add_rows(half_at, start, base, back):
    count, u, r = base.shape
    group = 16
    rows = pl.BlockSpec((group, u // 2, r), lambda i, at: (start // group + i, at[0], 0))
    return pl.pallas_call(
        add_kernel,
        out_shape=jax.ShapeDtypeStruct((count, u, r), F32),
        grid_spec=pltpu.PrefetchScalarGridSpec(
            num_scalar_prefetch=1,
            grid=(back.shape[0] // group,),
            in_specs=[rows, pl.BlockSpec((group, u // 2, r), lambda i, at: (i, 0, 0))],
            out_specs=rows,
        ),
        input_output_aliases={1: 0},
        compiler_params=pltpu.CompilerParams(vmem_limit_bytes=16 * MIB),
        cost_estimate=pl.CostEstimate(flops=0, bytes_accessed=3 * MIB, transcendentals=0),
        name="add_rows",
    )(half_at, base, back)


def after(arrays, *others):
    return lax.optimization_barrier((tuple(arrays), others))[0]


def body(
    vectors,
    sigma,
    near_blocks,
    near_index,
    radiate,
    interp_one,
    interp_two,
    trans_one,
    level1_source,
    level1_offset,
    trans_two,
    level2_source,
    level2_offset,
):
    x = vectors[0]
    count = x.shape[0]
    boxes = lax.axis_size("box")
    k2 = interp_two.shape[1]
    hops = routes(boxes)
    swap = [(i, i ^ 1) for i in range(boxes)]
    partners = [(0, 1), (1, 0)]
    core = lax.rem(lax.axis_index("box"), 2).astype(jnp.int32)
    shift = lax.axis_index("shift").astype(jnp.int32)
    lists = (
        near_index.reshape(-1),
        level1_source.reshape(-1),
        level1_offset.reshape(-1),
        radiate.T,
        (1 - shift).reshape(1),
        *translation_lists(trans_two, level2_source, level2_offset, x.shape[2]),
    )

    first_a, first_b = [
        lax.ppermute(half, BOTH, hops[0]) for half in (x[: count // 2], x[count // 2 :])
    ]
    mate = lax.ppermute(x, "box", swap)
    coarse, mine = upward(x, radiate, interp_one, interp_two)

    (first_a,) = after([first_a], coarse)
    partner_a = lax.ppermute(first_a, BOTH, hops[1])
    coarse, *lists = after([coarse, *lists], first_a)
    index, source, offset, turned_radiate, half_at, *translation = lists
    (gathered,) = exchange(coarse.reshape(boxes, k2 // boxes, -1))

    first_b, partner_a = after([first_b, partner_a], gathered)
    partner_b = lax.ppermute(first_b, BOTH, hops[1])
    last_a = lax.ppermute(partner_a, BOTH, hops[2])
    turned = translate(gathered, *translation)
    beside = patterns_beside(core.reshape(1), mate, first_a, first_b, radiate, interp_one)
    (turned,) = after([turned], beside, last_a)
    incoming, partner_mate_a, partner_mate_b, last_b = exchange(turned, partner_a, partner_b)
    incoming = incoming.reshape(k2, -1)

    (index,) = after([index], incoming)
    here = (
        x, mate, partner_a, partner_b, partner_mate_a, partner_mate_b, first_a, first_b, last_a, last_b
    )
    early = count // 2
    own_a, other_a = near_field(0, early, index, near_blocks, *here)
    back_a = lax.ppermute(other_a, "shift", partners)
    (index,) = after([index], other_a)
    own_b, other_b = near_field(early, count, index, near_blocks, *here)
    back_b = lax.ppermute(other_b, "shift", partners)
    source, offset = after([source, offset], other_b)
    local = local_field(
        source, offset, last_a, last_b, mine, beside, radiate, interp_one, interp_two, trans_one, incoming
    )
    base = leaf_fields(x, own_a, own_b, sigma, turned_radiate, interp_one, local)
    base = add_rows(half_at, 0, base, back_a)
    return add_rows(half_at, early, base, back_b)[None]


def solution(mesh):
    in_specs = (
        P("shift", "box", None, None),
        P("shift", None),
        P("box", None, "shift", None),
        P("box", None),
        P(),
        P(),
        P(),
        P(),
        P("box", None),
        P("box", None),
        P(None, "box"),
        P(),
        P(),
    )
    out_specs = P("shift", "box", None, None)
    return jax.shard_map(body, mesh=mesh, in_specs=in_specs, out_specs=out_specs, check_vma=False)
```

```python
import functools

import jax
import jax.numpy as jnp
from jax import lax
from jax.experimental import pallas as pl
from jax.experimental.pallas import tpu as pltpu
from jax.sharding import PartitionSpec as P

BF = jnp.bfloat16
F32 = jnp.float32
MIB = 1 << 20
ANY = pl.BlockSpec(memory_space=pl.ANY)
VMEM = pl.BlockSpec(memory_space=pltpu.VMEM)
BOTH = ("box", "shift")
DEPTH = 4


def dot(a, b):
    return jnp.dot(a, b, preferred_element_type=F32)


def dot_nt(a, b):
    return lax.dot_general(a, b, (((1,), (1,)), ((), ())), preferred_element_type=F32)


def routes(boxes):
    chips = boxes // 2

    def flat(chip, core, shift):
        return (chip % chips * 2 + core) * 2 + shift

    hops = ([], [], [])
    for chip in range(chips):
        for core in range(2):
            wraps = chip % DEPTH == (DEPTH - 1 if core else 0)
            beside = chip + (1 if core else -1)
            for shift in range(2):
                stops = [
                    flat(chip, core, shift),
                    flat(beside, 1 - core, 1 - shift if wraps else shift),
                    flat(chip, core, 1 - shift),
                    flat(beside, 1 - core, shift if wraps else 1 - shift),
                ]
                for hop in range(3):
                    hops[hop].append((stops[hop], stops[hop + 1]))
    return hops


def place():
    me = lax.axis_index("box")
    core = lax.rem(me, 2)
    depth = lax.rem(lax.div(me, 2), DEPTH)
    wraps = jnp.where(core == 0, depth == 0, depth == DEPTH - 1).astype(jnp.int32)
    return me, core, wraps


def exchange_kernel(chips, parts, x_ref, *refs):
    sources, refs = refs[:parts], refs[parts:]
    o_ref, refs = refs[0], refs[1:]
    targets, refs = refs[:parts], refs[parts:]
    held, send, recv, mate_send, mate_recv, local, part_send, part_recv = refs
    me, core, _ = place()
    shift = lax.axis_index("shift")
    chip = lax.div(me, 2)
    mate = me + 1 - 2 * core
    barrier = pltpu.get_barrier_semaphore()

    def greet(box, along):
        pl.semaphore_signal(
            barrier, inc=1, device_id=(box, along), device_id_type=pl.DeviceIdType.MESH
        )

    greet(mate, shift)

    @pl.loop(1, chips)
    def _(step):
        greet(lax.rem(chip + step, chips) * 2 + core, shift)

    own = pltpu.make_async_copy(x_ref.at[:, core], held.at[:, core], local)
    own.start()
    pl.semaphore_wait(barrier, chips)
    across = pltpu.make_async_remote_copy(
        x_ref.at[:, 1 - core],
        held.at[:, core],
        mate_send,
        mate_recv,
        device_id=(mate, shift),
        device_id_type=pl.DeviceIdType.MESH,
    )
    across.start()
    moves = [
        pltpu.make_async_remote_copy(
            sources[i],
            targets[i],
            part_send.at[i],
            part_recv.at[i],
            device_id=(mate, shift),
            device_id_type=pl.DeviceIdType.MESH,
        )
        for i in range(parts)
    ]
    for move in moves:
        move.start()
    own.wait()
    across.wait()

    @pl.loop(1, chips)
    def _(step):
        other = lax.rem(chip + step, chips)
        pltpu.make_async_remote_copy(
            held.at[other],
            o_ref.at[chip],
            send,
            recv,
            device_id=(other * 2 + core, shift),
            device_id_type=pl.DeviceIdType.MESH,
        ).start()

    own = pltpu.make_async_copy(held.at[chip], o_ref.at[chip], local)
    own.start()
    own.wait()
    rest = pl.ds(0, chips - 1)
    pltpu.make_async_copy(held.at[rest], held.at[rest], send).wait()
    pltpu.make_async_copy(o_ref.at[rest], o_ref.at[rest], recv).wait()
    for move in moves:
        move.wait()


def exchange(blocks, *parts):
    count, samples, r = blocks.shape
    shape = (count // 2, 2, samples, r)
    n = len(parts)
    blocks, *moved = pl.pallas_call(
        functools.partial(exchange_kernel, count // 2, n),
        out_shape=[jax.ShapeDtypeStruct(shape, BF)]
        + [jax.ShapeDtypeStruct(part.shape, BF) for part in parts],
        in_specs=[VMEM] + [ANY] * n,
        out_specs=[VMEM] + [ANY] * n,
        scratch_shapes=[pltpu.VMEM(shape, BF)]
        + [pltpu.SemaphoreType.DMA] * 5
        + [pltpu.SemaphoreType.DMA((max(n, 1),))] * 2,
        compiler_params=pltpu.CompilerParams(
            has_side_effects=True, collective_id=1 if n else 0, vmem_limit_bytes=56 * MIB
        ),
        cost_estimate=pl.CostEstimate(flops=0, bytes_accessed=80 * MIB, transcendentals=0),
        name="exchange",
    )(blocks.reshape(shape), *parts)
    return blocks.reshape(count, samples, r), *moved


def identity(n):
    shape = (n, n)
    same = lax.broadcasted_iota(jnp.int32, shape, 0) == lax.broadcasted_iota(jnp.int32, shape, 1)
    return same.astype(BF)


def two_parents(x_of, radiate, one_ref):
    total = None
    for pair in range(4):
        leaves = [
            dot(radiate, jnp.concatenate([x_of(o), x_of(8 + o)], axis=1)).astype(BF)
            for o in (2 * pair, 2 * pair + 1)
        ]
        lhs = jnp.concatenate([one_ref[2 * pair], one_ref[2 * pair + 1]], axis=1)
        term = dot(lhs, jnp.concatenate(leaves, axis=0))
        total = term if total is None else total + term
    return total


def upward_kernel(x_ref, radiate_ref, one_ref, two_ref, coarse_ref, patterns_ref, total):
    step = pl.program_id(0)
    upper = two_parents(lambda i: x_ref[i], radiate_ref[...], one_ref).astype(BF)
    r = x_ref.shape[2]
    left, right = upper[:, :r], upper[:, r:]
    term = dot(two_ref[0], left) + dot(two_ref[1], right)

    @pl.when(step == 0)
    def _():
        total[...] = term

    @pl.when(step > 0)
    def _():
        total[...] += term

    eye = identity(r)
    patterns_ref[0] = dot_nt(eye, left).astype(BF)
    patterns_ref[1] = dot_nt(eye, right).astype(BF)

    @pl.when(step == pl.num_programs(0) - 1)
    def _():
        coarse_ref[...] = total[...].astype(BF)


def upward(x, radiate, one, two):
    octants, k2, k1 = two.shape
    count, u, r = x.shape
    return pl.pallas_call(
        upward_kernel,
        grid=(octants // 2,),
        out_shape=[
            jax.ShapeDtypeStruct((k2, r), BF),
            jax.ShapeDtypeStruct((count // 8, r, k1), BF),
        ],
        in_specs=[
            pl.BlockSpec((16, u, r), lambda i: (i, 0, 0)),
            VMEM,
            VMEM,
            pl.BlockSpec((2, k2, k1), lambda i: (i, 0, 0)),
        ],
        out_specs=[
            pl.BlockSpec((k2, r), lambda i: (0, 0)),
            pl.BlockSpec((2, r, k1), lambda i: (i, 0, 0)),
        ],
        scratch_shapes=[pltpu.VMEM((k2, r), F32)],
        compiler_params=pltpu.CompilerParams(vmem_limit_bytes=56 * MIB),
        cost_estimate=pl.CostEstimate(flops=7_000_000_000, bytes_accessed=50 * MIB, transcendentals=0),
        name="upward",
    )(x, radiate, one, two)


def fill_patterns(x_of, patterns, at, radiate, one_ref):
    for pair in range(2):
        upper = two_parents(lambda i: x_of(16 * pair + i), radiate, one_ref).astype(BF)
        r = upper.shape[1] // 2
        eye = identity(r)
        patterns[at + 2 * pair] = dot_nt(eye, upper[:, :r]).astype(BF)
        patterns[at + 2 * pair + 1] = dot_nt(eye, upper[:, r:]).astype(BF)


def beside_kernel(_, mate_ref, first_ref, radiate_ref, one_ref, patterns_ref):
    step = pl.program_id(0)
    for when, ref in ((step < 2, mate_ref), (step >= 2, first_ref)):

        @pl.when(when)
        def _(ref=ref):
            fill_patterns(lambda i: ref[i], patterns_ref, 0, radiate_ref[...], one_ref)


def patterns_beside(core, mate, first, radiate, one):
    count, u, r = mate.shape
    _, k1, k0 = one.shape

    def where(i, core):
        towards = 4 * core[0]
        return (jnp.where(i < 2, 4 - towards + i, towards + i - 2), 0, 0)

    return pl.pallas_call(
        beside_kernel,
        out_shape=jax.ShapeDtypeStruct((3 * count // 8, r, k1), BF),
        grid_spec=pltpu.PrefetchScalarGridSpec(
            num_scalar_prefetch=1,
            grid=(4,),
            in_specs=[
                pl.BlockSpec((count // 2, u, r), lambda i, _: (jnp.minimum(i, 1), 0, 0)),
                pl.BlockSpec((count // 2, u, r), lambda i, _: (jnp.maximum(i - 2, 0), 0, 0)),
                VMEM,
                VMEM,
            ],
            out_specs=pl.BlockSpec((count // 16, r, k1), where),
        ),
        compiler_params=pltpu.CompilerParams(vmem_limit_bytes=56 * MIB),
        cost_estimate=pl.CostEstimate(flops=4_000_000_000, bytes_accessed=30 * MIB, transcendentals=0),
        name="patterns_beside",
    )(core, mate, first, radiate, one)


def translate_kernel(width, source_ref, offset_ref, rounds_ref, coarse_ref, weight_ref, out_ref):
    @pl.loop(0, out_ref.shape[0])
    def _(box):
        def four(step, total):
            for j in range(4):
                at = box * width + step * 4 + j
                total += weight_ref[offset_ref[at]] * coarse_ref[source_ref[at]].astype(F32)
            return total

        start = jnp.zeros(out_ref.shape[1:], F32)
        out_ref[box] = lax.fori_loop(0, rounds_ref[box], four, start).astype(BF)


def translation_lists(table, source, offset, columns):
    classes, samples = table.shape
    live = source >= 0
    rounds = (jnp.sum(live.astype(jnp.int32), axis=1) + 3) // 4
    weights = jnp.broadcast_to(
        jnp.pad(table, ((0, 1), (0, 0)))[:, :, None], (classes + 1, samples, columns)
    )
    return (
        jnp.where(live, source, 0).reshape(-1),
        jnp.where(live, offset, classes).reshape(-1),
        rounds,
        weights,
    )


def translate(coarse, source, offset, rounds, weights):
    return pl.pallas_call(
        functools.partial(translate_kernel, source.shape[0] // coarse.shape[0]),
        out_shape=jax.ShapeDtypeStruct(coarse.shape, BF),
        grid_spec=pltpu.PrefetchScalarGridSpec(
            num_scalar_prefetch=3, grid=(), in_specs=[VMEM, VMEM], out_specs=VMEM
        ),
        compiler_params=pltpu.CompilerParams(vmem_limit_bytes=16 * MIB),
        cost_estimate=pl.CostEstimate(flops=2_000_000_000, bytes_accessed=25 * MIB, transcendentals=0),
        name="translate",
    )(source, offset, rounds, coarse, weights)


def near_kernel(group, slots, start, index_ref, blocks_ref, *refs):
    sources, (own_ref, other_ref, held, sems) = refs[:-4], refs[-4:]
    step = pl.program_id(0)
    me, core, wraps = place()
    count = sources[0].shape[0]

    @pl.when(step == 0)
    def _():
        towards = 2 * core * count
        within = 2 * count - towards
        places = (
            (0, count),
            (0, within),
            (1, count),
            (1, within),
            (wraps, towards),
            (1 - wraps, towards),
        )
        copies = [
            pltpu.make_async_copy(src, held.at[kind, pl.ds(at, src.shape[0])], sems.at[i])
            for i, (src, (kind, at)) in enumerate(zip(sources, places))
        ]
        for copy in copies:
            copy.start()
        zero = jnp.zeros(held.shape[2:], BF)
        held[0, 3 * count] = zero
        held[1, 3 * count] = zero
        for copy in copies:
            copy.wait()

    base = me * count - count
    origin = start + step * group
    for b in range(group):
        total = None
        for pair in range(slots // 2):
            rows = []
            for i in range(2):
                at = index_ref[(origin + b) * slots + 2 * pair + i]
                at = jnp.where(at >= 0, at - base, 3 * count)
                rows.append(jnp.concatenate([held[0, at], held[1, at]], axis=1))
            lhs = jnp.concatenate([blocks_ref[b, 2 * pair], blocks_ref[b, 2 * pair + 1]], axis=1)
            term = dot(lhs, jnp.concatenate(rows, axis=0))
            total = term if total is None else total + term
        r = own_ref.shape[2]
        own_ref[b] = total[:, :r]
        other_ref[b] = total[:, r:].astype(BF)


def near_field(start, stop, index, blocks, *sources):
    count, slots, rows, u = blocks.shape
    r = sources[0].shape[2]
    group = 8
    out = pl.BlockSpec((group, rows, r), lambda i, *_: (i, 0, 0))
    return pl.pallas_call(
        functools.partial(near_kernel, group, slots, start),
        out_shape=[
            jax.ShapeDtypeStruct((stop - start, rows, r), F32),
            jax.ShapeDtypeStruct((stop - start, rows, r), BF),
        ],
        grid_spec=pltpu.PrefetchScalarGridSpec(
            num_scalar_prefetch=1,
            grid=((stop - start) // group,),
            in_specs=[
                pl.BlockSpec((group, slots, rows, u), lambda i, _: (start // group + i, 0, 0, 0))
            ]
            + [ANY] * len(sources),
            out_specs=[out, out],
            scratch_shapes=[
                pltpu.VMEM((2, 3 * count + 1, u, r), BF),
                pltpu.SemaphoreType.DMA((len(sources),)),
            ],
        ),
        compiler_params=pltpu.CompilerParams(vmem_limit_bytes=56 * MIB),
        cost_estimate=pl.CostEstimate(flops=3_000_000_000, bytes_accessed=20 * MIB, transcendentals=0),
        name="near_field",
    )(index, blocks, *sources)


def local_kernel(
    width, source_ref, offset_ref, last, mine, beside, radiate_ref, one_ref, two_ref,
    table_ref, incoming_ref, local_ref, held, patterns, flat, weights, across, sems,
):
    step = pl.program_id(0)
    me, core, wraps = place()
    count, u, r = held.shape
    parents = count // 8
    half = count // 2

    @pl.when(step == 0)
    def _():
        towards = 2 * core * parents
        within = pl.ds(2 * parents - towards, parents)
        center = pl.ds(parents, parents)
        copies = [
            pltpu.make_async_copy(mine, patterns.at[center], sems.at[0]),
            pltpu.make_async_copy(beside.at[within], patterns.at[within], sems.at[1]),
        ]
        for copy in copies:
            copy.start()
        flat[...] = dot_nt(identity(r), incoming_ref[...]).astype(BF)

        @pl.when(wraps == 0)
        def _():
            there = pl.ds(towards, parents)
            copy = pltpu.make_async_copy(beside.at[there], patterns.at[there], sems.at[2])
            copy.start()
            copy.wait()

        @pl.when(wraps == 1)
        def _():
            copy = pltpu.make_async_copy(last, held, sems.at[2])
            copy.start()
            copy.wait()

            @pl.loop(0, 2)
            def _(i):
                fill_patterns(
                    lambda k: held[i * half + k], patterns, towards + i * 4, radiate_ref[...], one_ref
                )

        for copy in copies:
            copy.wait()

    origin = me * parents - parents
    at = []
    for j in range(width):
        source = source_ref[step * width + j]
        live = source >= 0
        at.append(jnp.where(live, source - origin, parents))
        row = table_ref[pl.ds(offset_ref[step * width + j], 1), :]
        weights[pl.ds(j, 1), :] = row * live.astype(F32)

    @pl.loop(0, r // 16)
    def _(part):
        rows = pl.ds(pl.multiple_of(part * 16, 16), 16)
        total = None
        for j in range(width):
            term = weights[pl.ds(j, 1), :] * patterns[at[j], rows, :].astype(F32)
            total = term if total is None else total + term
        across[rows, :] = total

    local_ref[...] = (across[...] + dot(flat[...], two_ref[0])).astype(BF)


def local_field(source, offset, last, mine, beside, radiate, one, two, table, incoming):
    octants, k2, k1 = two.shape
    _, u, r = last.shape
    width = source.shape[0] // octants
    return pl.pallas_call(
        functools.partial(local_kernel, width),
        out_shape=jax.ShapeDtypeStruct((octants * r, k1), BF),
        grid_spec=pltpu.PrefetchScalarGridSpec(
            num_scalar_prefetch=2,
            grid=(octants,),
            in_specs=[ANY] * 3
            + [VMEM, VMEM, pl.BlockSpec((1, k2, k1), lambda i, *_: (i, 0, 0)), VMEM, VMEM],
            out_specs=pl.BlockSpec((r, k1), lambda i, *_: (i, 0)),
            scratch_shapes=[
                pltpu.VMEM((octants * 8, u, r), BF),
                pltpu.VMEM((3 * octants, r, k1), BF),
                pltpu.VMEM((r, k2), BF),
                pltpu.VMEM((width, k1), F32),
                pltpu.VMEM((r, k1), F32),
                pltpu.SemaphoreType.DMA((3,)),
            ],
        ),
        compiler_params=pltpu.CompilerParams(vmem_limit_bytes=56 * MIB),
        cost_estimate=pl.CostEstimate(flops=5_000_000_000, bytes_accessed=50 * MIB, transcendentals=0),
        name="local_field",
    )(source, offset, last, mine, beside, radiate, one, two, table, incoming)


def leaves_kernel(
    early, x_ref, a_ref, b_ref, sigma_ref, turned_ref, one_ref, local_ref, base_ref
):
    parents, _, u, r = x_ref.shape
    rows = u // 2
    shift = lax.axis_index("shift")
    own = pl.ds(pl.multiple_of(shift * rows, rows), rows)
    sig_re, sig_im = sigma_ref[0], sigma_ref[1]
    leaf_in = dot(local_ref[...], one_ref[0]).astype(BF)
    far = dot_nt(turned_ref[...], leaf_in)
    for c in range(parents):
        part = far[:, c * r : (c + 1) * r]
        field = x_ref[c, 0].astype(F32)
        real, imag = field[:rows], field[rows:]
        base_ref[c, 0, :rows] = part[:rows] - (sig_re * real - sig_im * imag)
        base_ref[c, 0, rows:] = part[rows:] - (sig_re * imag + sig_im * real)
        base_ref[c, 0, own] += a_ref[c, 0] if c < early else b_ref[c - early, 0]


def leaf_fields(x, own_a, own_b, sigma, turned, one, local):
    count, u, r = x.shape
    octants, k1, k0 = one.shape
    parents = count // octants
    early = own_a.shape[0] // octants

    def apart(array):
        return array.reshape(array.shape[0] // octants, octants, *array.shape[1:])

    def spec(array):
        return pl.BlockSpec((array.shape[0], 1, *array.shape[2:]), lambda i: (0, i, 0, 0))

    parts = [apart(array) for array in (x, own_a, own_b)]
    return pl.pallas_call(
        functools.partial(leaves_kernel, early),
        grid=(octants,),
        out_shape=jax.ShapeDtypeStruct((parents, octants, u, r), F32),
        in_specs=[spec(part) for part in parts]
        + [
            pl.BlockSpec(memory_space=pltpu.SMEM),
            VMEM,
            pl.BlockSpec((1, k1, k0), lambda i: (i, 0, 0)),
            VMEM,
        ],
        out_specs=spec(parts[0]),
        compiler_params=pltpu.CompilerParams(vmem_limit_bytes=56 * MIB),
        cost_estimate=pl.CostEstimate(flops=2_000_000_000, bytes_accessed=20 * MIB, transcendentals=0),
        name="leaf_fields",
    )(*parts, sigma.reshape(-1), turned, one, local).reshape(count, u, r)


def add_kernel(_, base_ref, back_ref, out_ref):
    out_ref[...] = base_ref[...] + back_ref[...].astype(F32)


def add_rows(half_at, start, base, back):
    count, u, r = base.shape
    group = 16
    rows = pl.BlockSpec((group, u // 2, r), lambda i, at: (start // group + i, at[0], 0))
    return pl.pallas_call(
        add_kernel,
        out_shape=jax.ShapeDtypeStruct((count, u, r), F32),
        grid_spec=pltpu.PrefetchScalarGridSpec(
            num_scalar_prefetch=1,
            grid=(back.shape[0] // group,),
            in_specs=[rows, pl.BlockSpec((group, u // 2, r), lambda i, at: (i, 0, 0))],
            out_specs=rows,
        ),
        input_output_aliases={1: 0},
        compiler_params=pltpu.CompilerParams(vmem_limit_bytes=16 * MIB),
        cost_estimate=pl.CostEstimate(flops=0, bytes_accessed=3 * MIB, transcendentals=0),
        name="add_rows",
    )(half_at, base, back)


def after(arrays, *others):
    return lax.optimization_barrier((tuple(arrays), others))[0]


def body(
    vectors,
    sigma,
    near_blocks,
    near_index,
    radiate,
    interp_one,
    interp_two,
    trans_one,
    level1_source,
    level1_offset,
    trans_two,
    level2_source,
    level2_offset,
):
    x = vectors[0]
    count = x.shape[0]
    boxes = lax.axis_size("box")
    k2 = interp_two.shape[1]
    hops = routes(boxes)
    swap = [(i, i ^ 1) for i in range(boxes)]
    partners = [(0, 1), (1, 0)]
    core = lax.rem(lax.axis_index("box"), 2).astype(jnp.int32)
    shift = lax.axis_index("shift").astype(jnp.int32)
    lists = (
        near_index.reshape(-1),
        level1_source.reshape(-1),
        level1_offset.reshape(-1),
        radiate.T,
        (1 - shift).reshape(1),
        *translation_lists(trans_two, level2_source, level2_offset, x.shape[2]),
    )

    first = lax.ppermute(x, BOTH, hops[0])
    mate = lax.ppermute(x, "box", swap)
    coarse, mine = upward(x, radiate, interp_one, interp_two)

    (first,) = after([first], coarse)
    partner = lax.ppermute(first, BOTH, hops[1])
    beside = patterns_beside(core.reshape(1), mate, first, radiate, interp_one)
    coarse, *lists = after([coarse, *lists], beside)
    index, source, offset, turned_radiate, half_at, *translation = lists
    (gathered,) = exchange(coarse.reshape(boxes, k2 // boxes, -1))

    (partner,) = after([partner], gathered)
    last = lax.ppermute(partner, BOTH, hops[2])
    turned = translate(gathered, *translation)
    incoming, partner_mate = exchange(turned, partner)
    incoming = incoming.reshape(k2, -1)

    (index,) = after([index], incoming)
    here = (x, mate, partner, partner_mate, first, last)
    early = count // 2
    own_a, other_a = near_field(0, early, index, near_blocks, *here)
    back_a = lax.ppermute(other_a, "shift", partners)
    (index,) = after([index], other_a)
    own_b, other_b = near_field(early, count, index, near_blocks, *here)
    back_b = lax.ppermute(other_b, "shift", partners)
    source, offset = after([source, offset], other_b)
    local = local_field(
        source, offset, last, mine, beside, radiate, interp_one, interp_two, trans_one, incoming
    )
    base = leaf_fields(x, own_a, own_b, sigma, turned_radiate, interp_one, local)
    base = add_rows(half_at, 0, base, back_a)
    return add_rows(half_at, early, base, back_b)[None]


def solution(mesh):
    in_specs = (
        P("shift", "box", None, None),
        P("shift", None),
        P("box", None, "shift", None),
        P("box", None),
        P(),
        P(),
        P(),
        P(),
        P("box", None),
        P("box", None),
        P(None, "box"),
        P(),
        P(),
    )
    out_specs = P("shift", "box", None, None)
    return jax.shard_map(body, mesh=mesh, in_specs=in_specs, out_specs=out_specs, check_vma=False)
```

```python
import functools

import jax
import jax.numpy as jnp
from jax import lax
from jax.experimental import pallas as pl
from jax.experimental.pallas import tpu as pltpu
from jax.sharding import PartitionSpec as P

BF = jnp.bfloat16
F32 = jnp.float32
MIB = 1 << 20
ANY = pl.BlockSpec(memory_space=pl.ANY)
VMEM = pl.BlockSpec(memory_space=pltpu.VMEM)
BOTH = ("box", "shift")
DEPTH = 4


def dot(a, b):
    return jnp.dot(a, b, preferred_element_type=F32)


def dot_nt(a, b):
    return lax.dot_general(a, b, (((1,), (1,)), ((), ())), preferred_element_type=F32)


def routes(boxes):
    chips = boxes // 2

    def flat(chip, core, shift):
        return (chip % chips * 2 + core) * 2 + shift

    hops = ([], [], [])
    for chip in range(chips):
        for core in range(2):
            wraps = chip % DEPTH == (DEPTH - 1 if core else 0)
            beside = chip + (1 if core else -1)
            for shift in range(2):
                stops = [
                    flat(chip, core, shift),
                    flat(beside, 1 - core, 1 - shift if wraps else shift),
                    flat(chip, core, 1 - shift),
                    flat(beside, 1 - core, shift if wraps else 1 - shift),
                ]
                for hop in range(3):
                    hops[hop].append((stops[hop], stops[hop + 1]))
    return hops


def place():
    me = lax.axis_index("box")
    core = lax.rem(me, 2)
    depth = lax.rem(lax.div(me, 2), DEPTH)
    wraps = jnp.where(core == 0, depth == 0, depth == DEPTH - 1).astype(jnp.int32)
    return me, core, wraps


def exchange_kernel(chips, parts, x_ref, *refs):
    sources, refs = refs[:parts], refs[parts:]
    o_ref, refs = refs[0], refs[1:]
    to_mate, refs = refs[:parts], refs[parts:]
    to_neighbour, refs = refs[:parts], refs[parts:]
    held, send, recv, mate_send, mate_recv, local, part_send, part_recv = refs
    me, core, wraps = place()
    shift = lax.axis_index("shift")
    chip = lax.div(me, 2)
    mate = me + 1 - 2 * core
    beside = lax.rem(chip + chips - 1 + 2 * core, chips) * 2 + 1 - core
    beside_shift = shift + wraps * (1 - 2 * shift)
    barrier = pltpu.get_barrier_semaphore()

    def greet(box, along):
        pl.semaphore_signal(
            barrier, inc=1, device_id=(box, along), device_id_type=pl.DeviceIdType.MESH
        )

    greet(mate, shift)
    if parts:
        greet(beside, beside_shift)

    @pl.loop(1, chips)
    def _(step):
        greet(lax.rem(chip + step, chips) * 2 + core, shift)

    own = pltpu.make_async_copy(x_ref.at[:, core], held.at[:, core], local)
    own.start()
    pl.semaphore_wait(barrier, chips + (1 if parts else 0))
    across = pltpu.make_async_remote_copy(
        x_ref.at[:, 1 - core],
        held.at[:, core],
        mate_send,
        mate_recv,
        device_id=(mate, shift),
        device_id_type=pl.DeviceIdType.MESH,
    )
    across.start()
    moves = []
    for i in range(parts):
        for j, (ref, device) in enumerate(
            ((to_neighbour[i], (beside, beside_shift)), (to_mate[i], (mate, shift)))
        ):
            move = pltpu.make_async_remote_copy(
                sources[i],
                ref,
                part_send.at[2 * i + j],
                part_recv.at[2 * i + j],
                device_id=device,
                device_id_type=pl.DeviceIdType.MESH,
            )
            move.start()
            moves.append(move)
    own.wait()
    across.wait()

    @pl.loop(1, chips)
    def _(step):
        other = lax.rem(chip + step, chips)
        pltpu.make_async_remote_copy(
            held.at[other],
            o_ref.at[chip],
            send,
            recv,
            device_id=(other * 2 + core, shift),
            device_id_type=pl.DeviceIdType.MESH,
        ).start()

    own = pltpu.make_async_copy(held.at[chip], o_ref.at[chip], local)
    own.start()
    own.wait()
    rest = pl.ds(0, chips - 1)
    pltpu.make_async_copy(held.at[rest], held.at[rest], send).wait()
    pltpu.make_async_copy(o_ref.at[rest], o_ref.at[rest], recv).wait()
    for move in moves:
        move.wait()


def exchange(blocks, *parts):
    count, samples, r = blocks.shape
    shape = (count // 2, 2, samples, r)
    n = len(parts)
    blocks, *moved = pl.pallas_call(
        functools.partial(exchange_kernel, count // 2, n),
        out_shape=[jax.ShapeDtypeStruct(shape, BF)]
        + [jax.ShapeDtypeStruct(part.shape, BF) for part in parts] * 2,
        in_specs=[VMEM] + [ANY] * n,
        out_specs=[VMEM] + [ANY] * (2 * n),
        scratch_shapes=[pltpu.VMEM(shape, BF)]
        + [pltpu.SemaphoreType.DMA] * 5
        + [pltpu.SemaphoreType.DMA((max(2 * n, 1),))] * 2,
        compiler_params=pltpu.CompilerParams(
            has_side_effects=True, collective_id=1 if n else 0, vmem_limit_bytes=56 * MIB
        ),
        cost_estimate=pl.CostEstimate(flops=0, bytes_accessed=80 * MIB, transcendentals=0),
        name="exchange",
    )(blocks.reshape(shape), *parts)
    return blocks.reshape(count, samples, r), *moved


def identity(n):
    shape = (n, n)
    same = lax.broadcasted_iota(jnp.int32, shape, 0) == lax.broadcasted_iota(jnp.int32, shape, 1)
    return same.astype(BF)


def two_parents(x_of, radiate, one_ref):
    total = None
    for pair in range(4):
        leaves = [
            dot(radiate, jnp.concatenate([x_of(o), x_of(8 + o)], axis=1)).astype(BF)
            for o in (2 * pair, 2 * pair + 1)
        ]
        lhs = jnp.concatenate([one_ref[2 * pair], one_ref[2 * pair + 1]], axis=1)
        term = dot(lhs, jnp.concatenate(leaves, axis=0))
        total = term if total is None else total + term
    return total


def upward_kernel(x_ref, radiate_ref, one_ref, two_ref, coarse_ref, patterns_ref, total):
    step = pl.program_id(0)
    upper = two_parents(lambda i: x_ref[i], radiate_ref[...], one_ref).astype(BF)
    r = x_ref.shape[2]
    left, right = upper[:, :r], upper[:, r:]
    term = dot(two_ref[0], left) + dot(two_ref[1], right)

    @pl.when(step == 0)
    def _():
        total[...] = term

    @pl.when(step > 0)
    def _():
        total[...] += term

    eye = identity(r)
    patterns_ref[0] = dot_nt(eye, left).astype(BF)
    patterns_ref[1] = dot_nt(eye, right).astype(BF)

    @pl.when(step == pl.num_programs(0) - 1)
    def _():
        coarse_ref[...] = total[...].astype(BF)


def upward(x, radiate, one, two):
    octants, k2, k1 = two.shape
    count, u, r = x.shape
    return pl.pallas_call(
        upward_kernel,
        grid=(octants // 2,),
        out_shape=[
            jax.ShapeDtypeStruct((k2, r), BF),
            jax.ShapeDtypeStruct((count // 8, r, k1), BF),
        ],
        in_specs=[
            pl.BlockSpec((16, u, r), lambda i: (i, 0, 0)),
            VMEM,
            VMEM,
            pl.BlockSpec((2, k2, k1), lambda i: (i, 0, 0)),
        ],
        out_specs=[
            pl.BlockSpec((k2, r), lambda i: (0, 0)),
            pl.BlockSpec((2, r, k1), lambda i: (i, 0, 0)),
        ],
        scratch_shapes=[pltpu.VMEM((k2, r), F32)],
        compiler_params=pltpu.CompilerParams(vmem_limit_bytes=56 * MIB),
        cost_estimate=pl.CostEstimate(flops=7_000_000_000, bytes_accessed=50 * MIB, transcendentals=0),
        name="upward",
    )(x, radiate, one, two)


def fill_patterns(x_of, patterns, at, radiate, one_ref):
    for pair in range(2):
        upper = two_parents(lambda i: x_of(16 * pair + i), radiate, one_ref).astype(BF)
        r = upper.shape[1] // 2
        eye = identity(r)
        patterns[at + 2 * pair] = dot_nt(eye, upper[:, :r]).astype(BF)
        patterns[at + 2 * pair + 1] = dot_nt(eye, upper[:, r:]).astype(BF)


def beside_kernel(_, mate_ref, a_ref, b_ref, radiate_ref, one_ref, patterns_ref):
    step = pl.program_id(0)
    for when, ref in ((step < 2, mate_ref), (step == 2, a_ref), (step == 3, b_ref)):

        @pl.when(when)
        def _(ref=ref):
            fill_patterns(lambda i: ref[i], patterns_ref, 0, radiate_ref[...], one_ref)


def patterns_beside(core, mate, first_a, first_b, radiate, one):
    count, u, r = mate.shape
    _, k1, k0 = one.shape

    def where(i, core):
        towards = 4 * core[0]
        return (jnp.where(i < 2, 4 - towards + i, towards + jnp.where(i == 2, 1 - core[0], core[0])), 0, 0)

    whole = pl.BlockSpec((count // 2, u, r), lambda i, _: (0, 0, 0))
    return pl.pallas_call(
        beside_kernel,
        out_shape=jax.ShapeDtypeStruct((3 * count // 8, r, k1), BF),
        grid_spec=pltpu.PrefetchScalarGridSpec(
            num_scalar_prefetch=1,
            grid=(4,),
            in_specs=[
                pl.BlockSpec((count // 2, u, r), lambda i, _: (jnp.minimum(i, 1), 0, 0)),
                whole,
                whole,
                VMEM,
                VMEM,
            ],
            out_specs=pl.BlockSpec((count // 16, r, k1), where),
        ),
        compiler_params=pltpu.CompilerParams(vmem_limit_bytes=56 * MIB),
        cost_estimate=pl.CostEstimate(flops=4_000_000_000, bytes_accessed=30 * MIB, transcendentals=0),
        name="patterns_beside",
    )(core, mate, first_a, first_b, radiate, one)


def translate_kernel(width, source_ref, offset_ref, rounds_ref, coarse_ref, weight_ref, out_ref):
    @pl.loop(0, out_ref.shape[0])
    def _(box):
        def four(step, total):
            for j in range(4):
                at = box * width + step * 4 + j
                total += weight_ref[offset_ref[at]] * coarse_ref[source_ref[at]].astype(F32)
            return total

        start = jnp.zeros(out_ref.shape[1:], F32)
        out_ref[box] = lax.fori_loop(0, rounds_ref[box], four, start).astype(BF)


def translation_lists(table, source, offset, columns):
    classes, samples = table.shape
    live = source >= 0
    rounds = (jnp.sum(live.astype(jnp.int32), axis=1) + 3) // 4
    weights = jnp.broadcast_to(
        jnp.pad(table, ((0, 1), (0, 0)))[:, :, None], (classes + 1, samples, columns)
    )
    return (
        jnp.where(live, source, 0).reshape(-1),
        jnp.where(live, offset, classes).reshape(-1),
        rounds,
        weights,
    )


def translate(coarse, source, offset, rounds, weights):
    return pl.pallas_call(
        functools.partial(translate_kernel, source.shape[0] // coarse.shape[0]),
        out_shape=jax.ShapeDtypeStruct(coarse.shape, BF),
        grid_spec=pltpu.PrefetchScalarGridSpec(
            num_scalar_prefetch=3, grid=(), in_specs=[VMEM, VMEM], out_specs=VMEM
        ),
        compiler_params=pltpu.CompilerParams(vmem_limit_bytes=16 * MIB),
        cost_estimate=pl.CostEstimate(flops=2_000_000_000, bytes_accessed=25 * MIB, transcendentals=0),
        name="translate",
    )(source, offset, rounds, coarse, weights)


def near_kernel(group, slots, part, index_ref, halves_ref, blocks_ref, *refs):
    sources, (own_ref, other_ref, held, sems) = refs[:-4], refs[-4:]
    step = pl.program_id(0)
    me, core, wraps = place()
    count = sources[0].shape[0]
    half = count // 2

    @pl.when(step == 0)
    def _():
        towards = 2 * core * count
        within = 2 * count - towards
        upper, lower = half * (1 - core), half * core
        places = (
            (0, count),
            (0, within),
            (1, count + lower),
            (1, count + upper),
            (1, within + upper),
            (1, within + lower),
            (wraps, towards + upper),
            (1 - wraps, towards + upper),
            (wraps, towards + lower),
            (1 - wraps, towards + lower),
        )
        copies = [
            pltpu.make_async_copy(src, held.at[kind, pl.ds(at, src.shape[0])], sems.at[i])
            for i, (src, (kind, at)) in enumerate(zip(sources, places))
        ]
        for copy in copies:
            copy.start()
        zero = jnp.zeros(held.shape[2:], BF)
        held[0, 3 * count] = zero
        held[1, 3 * count] = zero
        for copy in copies:
            copy.wait()

    base = me * count - count
    origin = halves_ref[part] * half + step * group
    for b in range(group):
        total = None
        for pair in range(slots // 2):
            rows = []
            for i in range(2):
                at = index_ref[(origin + b) * slots + 2 * pair + i]
                at = jnp.where(at >= 0, at - base, 3 * count)
                rows.append(jnp.concatenate([held[0, at], held[1, at]], axis=1))
            lhs = jnp.concatenate([blocks_ref[b, 2 * pair], blocks_ref[b, 2 * pair + 1]], axis=1)
            term = dot(lhs, jnp.concatenate(rows, axis=0))
            total = term if total is None else total + term
        r = own_ref.shape[2]
        own_ref[b] = total[:, :r]
        other_ref[b] = total[:, r:].astype(BF)


def near_field(part, halves, index, blocks, *sources):
    count, slots, rows, u = blocks.shape
    r = sources[0].shape[2]
    group = 8
    steps = count // 2 // group
    out = pl.BlockSpec((group, rows, r), lambda i, *_: (i, 0, 0))
    return pl.pallas_call(
        functools.partial(near_kernel, group, slots, part),
        out_shape=[
            jax.ShapeDtypeStruct((count // 2, rows, r), F32),
            jax.ShapeDtypeStruct((count // 2, rows, r), BF),
        ],
        grid_spec=pltpu.PrefetchScalarGridSpec(
            num_scalar_prefetch=2,
            grid=(steps,),
            in_specs=[
                pl.BlockSpec((group, slots, rows, u), lambda i, _, h: (h[part] * steps + i, 0, 0, 0))
            ]
            + [ANY] * len(sources),
            out_specs=[out, out],
            scratch_shapes=[
                pltpu.VMEM((2, 3 * count + 1, u, r), BF),
                pltpu.SemaphoreType.DMA((len(sources),)),
            ],
        ),
        compiler_params=pltpu.CompilerParams(vmem_limit_bytes=56 * MIB),
        cost_estimate=pl.CostEstimate(flops=3_000_000_000, bytes_accessed=20 * MIB, transcendentals=0),
        name="near_field",
    )(index, halves, blocks, *sources)


def local_step(
    width, step, source_ref, offset_ref, last_a, last_b, mine, beside, radiate_ref, one_ref, two_ref,
    table_ref, incoming_ref, held, patterns, flat, weights, across, local, sems,
):
    me, core, wraps = place()
    count, u, r = held.shape
    parents = count // 8
    half = count // 2

    @pl.when(step == 0)
    def _():
        towards = 2 * core * parents
        within = pl.ds(2 * parents - towards, parents)
        center = pl.ds(parents, parents)
        copies = [
            pltpu.make_async_copy(mine, patterns.at[center], sems.at[0]),
            pltpu.make_async_copy(beside.at[within], patterns.at[within], sems.at[1]),
        ]
        for copy in copies:
            copy.start()
        flat[...] = dot_nt(identity(r), incoming_ref[...]).astype(BF)

        @pl.when(wraps == 0)
        def _():
            there = pl.ds(towards, parents)
            copy = pltpu.make_async_copy(beside.at[there], patterns.at[there], sems.at[2])
            copy.start()
            copy.wait()

        @pl.when(wraps == 1)
        def _():
            halves = [
                pltpu.make_async_copy(last_a, held.at[pl.ds(half * (1 - core), half)], sems.at[2]),
                pltpu.make_async_copy(last_b, held.at[pl.ds(half * core, half)], sems.at[3]),
            ]
            for copy in halves:
                copy.start()
            for copy in halves:
                copy.wait()

            @pl.loop(0, 2)
            def _(i):
                fill_patterns(
                    lambda k: held[i * half + k], patterns, towards + i * 4, radiate_ref[...], one_ref
                )

        for copy in copies:
            copy.wait()

    origin = me * parents - parents
    at = []
    for j in range(width):
        source = source_ref[step * width + j]
        live = source >= 0
        at.append(jnp.where(live, source - origin, parents))
        row = table_ref[pl.ds(offset_ref[step * width + j], 1), :]
        weights[pl.ds(j, 1), :] = row * live.astype(F32)

    @pl.loop(0, r // 16)
    def _(part):
        rows = pl.ds(pl.multiple_of(part * 16, 16), 16)
        total = None
        for j in range(width):
            term = weights[pl.ds(j, 1), :] * patterns[at[j], rows, :].astype(F32)
            total = term if total is None else total + term
        across[rows, :] = total

    local[pl.ds(pl.multiple_of(step * r, r), r), :] = (
        across[...] + dot(flat[...], two_ref[0])
    ).astype(BF)


def downward_kernel(
    width, source_ref, offset_ref, x_ref, last_a, last_b, mine, beside, a_ref, b_ref, sigma_ref,
    radiate_ref, turned_ref, one_ref, two_ref, table_ref, incoming_ref, base_ref,
    held, patterns, flat, weights, across, local, sems,
):
    step = pl.program_id(0)
    parents, _, u, r = x_ref.shape
    rows = u // 2

    @pl.when(step < parents)
    def _():
        local_step(
            width, step, source_ref, offset_ref, last_a, last_b, mine, beside, radiate_ref, one_ref,
            two_ref, table_ref, incoming_ref, held, patterns, flat, weights, across, local, sems,
        )

    @pl.when(step >= parents)
    def _():
        core = lax.rem(lax.axis_index("box"), 2)
        own = pl.ds(pl.multiple_of(lax.axis_index("shift") * rows, rows), rows)
        sig_re, sig_im = sigma_ref[0], sigma_ref[1]
        leaf_in = dot(local[...], one_ref[step - parents]).astype(BF)
        far = dot_nt(turned_ref[...], leaf_in)
        for c in range(parents):
            part = far[:, c * r : (c + 1) * r]
            field = x_ref[c, 0].astype(F32)
            real, imag = field[:rows], field[rows:]
            base_ref[c, 0, :rows] = part[:rows] - (sig_re * real - sig_im * imag)
            base_ref[c, 0, rows:] = part[rows:] - (sig_re * imag + sig_im * real)
            at = c % (parents // 2)
            in_a = core == (1 if c < parents // 2 else 0)
            base_ref[c, 0, own] += jnp.where(in_a, a_ref[at, 0], b_ref[at, 0])


def downward(
    source, offset, x, last_a, last_b, mine, beside, own_a, own_b, sigma, radiate, turned, one, two,
    table, incoming,
):
    octants, k2, k1 = two.shape
    count, u, r = x.shape
    parents = count // 8
    width = source.shape[0] // parents

    def child(i, *_):
        return (0, jnp.maximum(i - parents, 0), 0, 0)

    near = pl.BlockSpec((parents // 2, 1, u // 2, r), child)
    box = pl.BlockSpec((parents, 1, u, r), child)
    return pl.pallas_call(
        functools.partial(downward_kernel, width),
        out_shape=jax.ShapeDtypeStruct((parents, 8, u, r), F32),
        grid_spec=pltpu.PrefetchScalarGridSpec(
            num_scalar_prefetch=2,
            grid=(parents + 8,),
            in_specs=[
                box,
                ANY,
                ANY,
                ANY,
                ANY,
                near,
                near,
                pl.BlockSpec(memory_space=pltpu.SMEM),
                VMEM,
                VMEM,
                VMEM,
                pl.BlockSpec((1, k2, k1), lambda i, *_: (jnp.minimum(i, parents - 1), 0, 0)),
                VMEM,
                VMEM,
            ],
            out_specs=box,
            scratch_shapes=[
                pltpu.VMEM((count, u, r), BF),
                pltpu.VMEM((3 * parents, r, k1), BF),
                pltpu.VMEM((r, k2), BF),
                pltpu.VMEM((width, k1), F32),
                pltpu.VMEM((r, k1), F32),
                pltpu.VMEM((parents * r, k1), BF),
                pltpu.SemaphoreType.DMA((4,)),
            ],
        ),
        compiler_params=pltpu.CompilerParams(vmem_limit_bytes=56 * MIB),
        cost_estimate=pl.CostEstimate(flops=9_000_000_000, bytes_accessed=80 * MIB, transcendentals=0),
        name="downward",
    )(
        source, offset, x.reshape(parents, 8, u, r), last_a, last_b, mine, beside,
        own_a.reshape(parents // 2, 8, u // 2, r), own_b.reshape(parents // 2, 8, u // 2, r),
        sigma.reshape(-1), radiate, turned, one, two, table, incoming,
    ).reshape(count, u, r)


def add_kernel(_, base_ref, back_ref, out_ref):
    out_ref[...] = base_ref[...] + back_ref[...].astype(F32)


def add_rows(where, base, back):
    count, u, r = base.shape
    group = count // 4
    rows = pl.BlockSpec((group, u // 2, r), lambda i, at: (at[0] * 2 + i, at[1], 0))
    return pl.pallas_call(
        add_kernel,
        out_shape=jax.ShapeDtypeStruct((count, u, r), F32),
        grid_spec=pltpu.PrefetchScalarGridSpec(
            num_scalar_prefetch=1,
            grid=(2,),
            in_specs=[rows, pl.BlockSpec((group, u // 2, r), lambda i, at: (i, 0, 0))],
            out_specs=rows,
        ),
        input_output_aliases={1: 0},
        compiler_params=pltpu.CompilerParams(vmem_limit_bytes=16 * MIB),
        cost_estimate=pl.CostEstimate(flops=0, bytes_accessed=3 * MIB, transcendentals=0),
        name="add_rows",
    )(where, base, back)


def after(arrays, *others):
    return lax.optimization_barrier((tuple(arrays), others))[0]


def body(
    vectors,
    sigma,
    near_blocks,
    near_index,
    radiate,
    interp_one,
    interp_two,
    trans_one,
    level1_source,
    level1_offset,
    trans_two,
    level2_source,
    level2_offset,
):
    x = vectors[0]
    count = x.shape[0]
    boxes = lax.axis_size("box")
    k2 = interp_two.shape[1]
    hops = routes(boxes)
    swap = [(i, i ^ 1) for i in range(boxes)]
    partners = [(0, 1), (1, 0)]
    core = lax.rem(lax.axis_index("box"), 2).astype(jnp.int32)
    shift = lax.axis_index("shift").astype(jnp.int32)
    halves = jnp.stack([1 - core, core])
    lists = (
        near_index.reshape(-1),
        level1_source.reshape(-1),
        level1_offset.reshape(-1),
        radiate.T,
        halves,
        jnp.stack([1 - core, 1 - shift]),
        jnp.stack([core, 1 - shift]),
        *translation_lists(trans_two, level2_source, level2_offset, x.shape[2]),
    )

    first_a, first_b = [
        lax.ppermute(lax.dynamic_slice_in_dim(x, at * (count // 2), count // 2), BOTH, hops[0])
        for at in (core, 1 - core)
    ]
    mate = lax.ppermute(x, "box", swap)
    coarse, mine = upward(x, radiate, interp_one, interp_two)

    (first_a,) = after([first_a], coarse)
    partner_a = lax.ppermute(first_a, BOTH, hops[1])
    coarse, *lists = after([coarse, *lists], first_a)
    index, source, offset, turned_radiate, halves, where_a, where_b, *translation = lists
    (gathered,) = exchange(coarse.reshape(boxes, k2 // boxes, -1))

    first_b, partner_a = after([first_b, partner_a], gathered)
    partner_b = lax.ppermute(first_b, BOTH, hops[1])
    turned = translate(gathered, *translation)
    beside = patterns_beside(core.reshape(1), mate, first_a, first_b, radiate, interp_one)
    (turned,) = after([turned], beside)
    incoming, partner_mate_a, partner_mate_b, last_a, last_b = exchange(turned, partner_a, partner_b)
    incoming = incoming.reshape(k2, -1)
    (index,) = after([index], incoming)
    here = (x, mate, partner_a, partner_b, partner_mate_a, partner_mate_b, first_a, last_a)
    own_a, other_a = near_field(0, halves, index, near_blocks, *here)
    back_a = lax.ppermute(other_a, "shift", partners)
    (index,) = after([index], other_a)
    own_b, other_b = near_field(1, halves, index, near_blocks, *here, first_b, last_b)
    back_b = lax.ppermute(other_b, "shift", partners)
    base = downward(
        source, offset, x, last_a, last_b, mine, beside, own_a, own_b, sigma, radiate, turned_radiate,
        interp_one, interp_two, trans_one, incoming,
    )
    base = add_rows(where_a, base, back_a)
    return add_rows(where_b, base, back_b)[None]


def solution(mesh):
    in_specs = (
        P("shift", "box", None, None),
        P("shift", None),
        P("box", None, "shift", None),
        P("box", None),
        P(),
        P(),
        P(),
        P(),
        P("box", None),
        P("box", None),
        P(None, "box"),
        P(),
        P(),
    )
    out_specs = P("shift", "box", None, None)
    return jax.shard_map(body, mesh=mesh, in_specs=in_specs, out_specs=out_specs, check_vma=False)
```
